32 devices in a mesh: gx: 4 (over y, x), gy: 8 (over z, core).
Axes of the slice: x: 2, y: 2, z: 4, core: 2. Of those that a mesh axis runs over, the one named last changes fastest.
Arguments:
- right_side: float32 [70, 96, 1024], P(None, 'gx', 'gy'), may hold values from -6 to 6
- helm_coef: float32 [70, 96, 1024], P(None, 'gx', 'gy'), may hold values from 0.5 to 4
- vert_coef: float32 [71], replicated, may hold values from 1 to 10
- block_inverse: float32 [4, 5, 14, 14], replicated, may hold values from -0.1 to 0.45, as said below
- edge_flip: int32 [4, 8, 4], P('gx', 'gy'), may hold values 0 or 1
Outputs:
- correction: float32 [70, 96, 1024], P(None, 'gx', 'gy')
The draws below stay inside these ranges and needn't reach their ends.
Inputs may be any that keep to these rules, and one draw needn't show every extreme that they name: `block_inverse`: each block's diagonal entries are positive and larger than the off-diagonal ones.
All inputs are finite; a program needn't handle non-finite values. No bound on the sum of `edge_flip` on one device may be relied on, other than what follows from the above.
Results may differ from the reference program's by a relative error of at most 0.0001.
Values sent between devices are 32-bit elements; how exact they have to be, the bound alone decides.
A program may use at most 128 MiB of HBM per device.

```python
import math
import jax
import jax.numpy as jnp
from jax import lax

NZ = 70
BLK = 14
NBLK = 5
LEVELS = 4
NX = 96
NY = 1024
N_GX = 4
N_GY = 8


def draw_block_inverse(key, part):
    key = jax.random.fold_in(key, 7)
    first, second = jax.random.split(key)
    diag = jax.random.uniform(first, (LEVELS, NBLK, BLK), jnp.float32, 0.25, 0.45)
    off = jnp.clip(0.02 * jax.random.normal(second, (LEVELS, NBLK, BLK, BLK), jnp.float32), -0.09, 0.09)
    eye = jnp.eye(BLK, dtype=jnp.float32)
    return off * (1.0 - eye) + diag[..., None] * eye


def with_ends(entries, own_key, least, high):
    spot = [jax.random.randint(jax.random.fold_in(own_key, axis), (), 0, length) for axis, length in enumerate(entries.shape)]
    longest = entries.shape.index(max(entries.shape))
    neighbour = spot[:longest] + [(spot[longest] + 1) % entries.shape[longest]] + spot[longest + 1:]
    return entries.at[tuple(spot)].set(least).at[tuple(neighbour)].set(high)


def block_levels(key, extent, shards, least, top_value):
    level = 1.0
    for dim, shards_of in shards:
        steps = jax.random.uniform(jax.random.fold_in(jax.random.fold_in(key, 6), dim), (shards_of,), jnp.float32, least / len(shards), top_value / len(shards))
        level = level * jnp.repeat(jnp.exp(steps), extent[dim] // shards_of).reshape((-1,) + (1,) * (len(extent) - 1 - dim))
    return level


def scatter_about(stream_key, extent, spread, most, cuts=(), kind=jnp.bfloat16):
    result = jax.random.normal(stream_key, extent, jnp.float32) * spread
    if len(cuts) > 0:
        result = block_levels(stream_key, extent, cuts, -0.22, 0.18) * result
    return jnp.clip(result, min=-most, max=most).astype(kind)


def setup_inputs(seed: int = 0) -> dict:
    splits = jax.random.split(jax.random.key(seed), 6)
    right_side = scatter_about(splits[0], (NZ, NX, NY), 1.0, 6.0, ((1, 4), (2, 8)), jnp.float32)
    helm_coef = jnp.clip(jnp.exp(math.log(4.0) - 2.0794415 * jax.random.uniform(splits[1], (NZ, NX, NY), jnp.float32) ** block_levels(splits[1], (NZ, NX, NY), ((1, 4), (2, 8)), -0.2, 0.2)), 0.5, 4.0)
    vert_coef = jnp.clip(jnp.exp(jax.random.uniform(splits[2], (NZ + 1,), jnp.float32, math.log(1.0), math.log(10.0))), 1.0, 10.0)
    block_inverse = draw_block_inverse(jax.random.fold_in(splits[5], 71), 0)
    edge_flip = with_ends((jax.random.randint(splits[4], (N_GX, N_GY, 4), 0, 2) < 1).astype(jnp.int32), jax.random.fold_in(splits[4], 1), 0, 1)
    return {"right_side": right_side, "helm_coef": helm_coef, "vert_coef": vert_coef, "block_inverse": block_inverse, "edge_flip": edge_flip}


def vertical(field, vert_coef):
    zero = jnp.zeros_like(field[:1])
    above = jnp.concatenate([field[1:], zero], axis=0)
    below = jnp.concatenate([zero, field[:-1]], axis=0)
    couple = vert_coef[:, None, None]
    return couple[1:] * (field - above) + couple[:-1] * (field - below)


def operate(field, coef, vert_coef, edge_flip):
    depth, rows, cols = field.shape
    tile_x = rows // N_GX
    tile_y = cols // N_GY
    tiles = field.reshape(depth, N_GX, tile_x, N_GY, tile_y)
    flips = edge_flip > 0
    low_x = jnp.roll(tiles[:, :, tile_x - 1], 1, axis=1)
    low_x = jnp.where(flips[None, :, :, 0, None], low_x[..., ::-1], low_x)
    high_x = jnp.roll(tiles[:, :, 0], -1, axis=1)
    high_x = jnp.where(flips[None, :, :, 1, None], high_x[..., ::-1], high_x)
    low_y = jnp.roll(tiles[..., tile_y - 1], 1, axis=3)
    low_y = jnp.where(flips[None, :, None, :, 2], low_y[:, :, ::-1, :], low_y)
    high_y = jnp.roll(tiles[..., 0], -1, axis=3)
    high_y = jnp.where(flips[None, :, None, :, 3], high_y[:, :, ::-1, :], high_y)
    minus_x = jnp.concatenate([low_x[:, :, None], tiles[:, :, :-1]], axis=2)
    plus_x = jnp.concatenate([tiles[:, :, 1:], high_x[:, :, None]], axis=2)
    minus_y = jnp.concatenate([low_y[..., None], tiles[..., :-1]], axis=4)
    plus_y = jnp.concatenate([tiles[..., 1:], high_y[..., None]], axis=4)
    beside = (minus_x + plus_x + minus_y + plus_y).reshape(depth, rows, cols)
    return (coef * field + 4.0 * field - beside + vertical(field, vert_coef)) * 0.0625


def apply_blocks(inverse, resid):
    shape = resid.shape
    blocks = resid.reshape(inverse.shape[0], BLK, -1)
    out = jnp.einsum("kab,kbn->kan", inverse, blocks, precision=lax.Precision.HIGHEST)
    return out.reshape(shape)


def restrict(field):
    depth, rows, cols = field.shape
    return field.reshape(depth, rows // 2, 2, cols // 2, 2).mean(axis=(2, 4))


def prolong(field):
    return jnp.repeat(jnp.repeat(field, 2, axis=1), 2, axis=2)


def cycle(level, source, coef, vert_coef, block_inverse, edge_flip):
    inverse = block_inverse[level]
    field = apply_blocks(inverse, source)
    if level == LEVELS - 1:
        for sweep in range(3):
            field = field + apply_blocks(inverse, source - operate(field, coef, vert_coef, edge_flip))
        return field
    field = field + apply_blocks(inverse, source - operate(field, coef, vert_coef, edge_flip))
    resid = source - operate(field, coef, vert_coef, edge_flip)
    coarse = cycle(level + 1, restrict(resid), restrict(coef), vert_coef, block_inverse, edge_flip)
    field = field + prolong(coarse)
    for sweep in range(2):
        field = field + apply_blocks(inverse, source - operate(field, coef, vert_coef, edge_flip))
    return field


def reference(right_side, helm_coef, vert_coef, block_inverse, edge_flip):
    return cycle(0, right_side, helm_coef, vert_coef, block_inverse, edge_flip)
```

```python
import functools
import jax
import jax.numpy as jnp
from jax import lax
from jax.experimental import pallas as pl
from jax.experimental.pallas import tpu as pltpu
from jax.sharding import PartitionSpec as P

BLK = 14
LEVELS = 4
LANES = 128
MESH = pl.DeviceIdType.MESH
BF = jnp.bfloat16
F32 = jnp.float32


def split2(x):
    hi = x.astype(BF).astype(F32)
    return hi, x - hi


def permute(x, matrix):
    depth = x.shape[0]
    hi, lo = split2(x)
    both = jnp.concatenate([hi, lo], axis=0).astype(BF)
    out = jnp.dot(both, matrix, preferred_element_type=F32)
    return out[:depth] + out[depth:]


def block_dot(binv, r):
    hi, lo = split2(r)
    cat = jnp.concatenate([hi, lo, hi, jnp.zeros((8, r.shape[1]), F32)], axis=0).astype(BF)
    return jnp.dot(binv, cat, preferred_element_type=F32)


def kernel(n_gx, n_gy, rows0, depth, flip_ref, s_in, c_in, kz_ref, binv_ref, out_ref,
           va0, va1, va2, va3, vb0, vb1, vb2, vb3, s0, s1, s2, s3, d0, d1, d2, d3,
           edge, held, px, py, resm, prom, send_sem, recv_sem):
    va, vb = (va0, va1, va2, va3), (vb0, vb1, vb2, vb3)
    src, dia = (s0, s1, s2, s3), (d0, d1, d2, d3)
    gx, gy = lax.axis_index("gx"), lax.axis_index("gy")
    peers = (
        (lax.rem(gx + n_gx - 1, n_gx), gy),
        (lax.rem(gx + 1, n_gx), gy),
        (gx, lax.rem(gy + n_gy - 1, n_gy)),
        (gx, lax.rem(gy + 1, n_gy)),
    )
    barrier = pltpu.get_barrier_semaphore()
    for peer in peers:
        pl.semaphore_signal(barrier, inc=1, device_id=peer, device_id_type=MESH)

    nrow = [rows0 >> l for l in range(LEVELS)]
    ncol = [LANES >> l for l in range(LEVELS)]
    lane = lax.broadcasted_iota(jnp.int32, (depth, LANES), 1)
    ki = lax.broadcasted_iota(jnp.int32, (LANES, LANES), 0)
    mi = lax.broadcasted_iota(jnp.int32, (LANES, LANES), 1)
    flips = [flip_ref[0, 0, s] > 0 for s in range(4)]

    def as_matrix(hit, value=1.0):
        return jnp.where(hit, value, 0.0).astype(F32).astype(BF)

    for l in range(LEVELS):
        r, c = nrow[l], ncol[l]
        for side in range(2):
            spot = jnp.where(flips[side], c - 1 - mi, mi)
            px[l, side] = as_matrix((ki == spot) & (mi < c))
        xm = mi >> 1
        from_low = (2 * jnp.where(flips[2], r - 1 - xm, xm) + c) & (LANES - 1)
        py[l, 0:LANES, :] = as_matrix((ki == from_low) & ((mi & 1) == 1) & (xm < r))
        xh = ((mi - c) & (LANES - 1)) >> 1
        from_high = 2 * jnp.where(flips[3], r - 1 - xh, xh) + 1
        py[l, LANES:, :] = as_matrix((ki == from_high) & ((mi & 1) == 0) & (xh < r))
    for l in range(LEVELS - 1):
        resm[l] = as_matrix(((ki >> 1) == mi) & (mi < ncol[l + 1]), 0.25)
        prom[l] = as_matrix(((mi >> 1) == ki) & (mi < ncol[l]))

    for l in range(LEVELS):
        for buf in (va[l], vb[l]):
            buf[0] = jnp.zeros((depth, LANES), F32)
            buf[nrow[l] + 1] = jnp.zeros((depth, LANES), F32)

    group = [4, 4, 6, 3]

    def each_group(l, body, carry=0):
        g = group[l] if nrow[l] % group[l] == 0 else 1
        trips = nrow[l] // g
        if trips == 1:
            return body(0, g, carry)
        return lax.fori_loop(0, trips, lambda i, acc: body(i * g, g, acc), carry)

    def extract(acc, row, x, c):
        turned = pltpu.roll(row, 2 * x + 1, 1)
        hit = (lane == 2 * x + 1) | (lane == ((2 * x + c) & (LANES - 1)))
        return jnp.where(hit, turned, acc)

    def ends(c):
        return (lane == 0) | (lane == c - 1)

    def insert(tile, x, c):
        return jnp.where(ends(c), pltpu.roll(tile, (LANES - 1) - 2 * x, 1), 0.0)

    def send(k, l, v):
        r = nrow[l]
        plan = ((v.at[1], 0, 1), (v.at[r], 1, 0), (edge, 2, 3), (edge, 3, 2))
        copies = []
        for ref, to, slot in plan:
            copies.append(pltpu.make_async_remote_copy(
                src_ref=ref, dst_ref=held.at[k, slot], send_sem=send_sem.at[k, slot],
                recv_sem=recv_sem.at[k, slot], device_id=peers[to], device_id_type=MESH))
            copies[-1].start()
        return copies

    up, down = kz_ref[0], kz_ref[1]

    def partial(l, v, x):
        c = ncol[l]
        mid = v[x + 1]
        r = src[l][x] - dia[l][x] * mid + (v[x] + v[x + 2])
        r = r + jnp.where(lane == 0, 0.0, pltpu.roll(mid, 1, 1))
        r = r + jnp.where(lane == c - 1, 0.0, pltpu.roll(mid, LANES - 1, 1))
        r = r + up * pltpu.roll(mid, depth - 1, 0) + down * pltpu.roll(mid, 1, 0)
        return r, mid

    def halos(k, l):
        low = permute(held[k, 0], px[l, 0])
        high = permute(held[k, 1], px[l, 1])
        beside = permute(jnp.concatenate([held[k, 2], held[k, 3]], axis=1), py[l])
        return low, high, beside

    count = [0]

    def from_zero(l, v):
        def body(x0, g, acc):
            rr = jnp.concatenate([src[l][x0 + j] for j in range(g)], axis=1)
            d = block_dot(binv_ref[l], rr)
            for j in range(g):
                row = d[:, j * LANES:(j + 1) * LANES]
                v[x0 + j + 1] = row
                acc = extract(acc, row, x0 + j, ncol[l])
            return acc
        edge[...] = each_group(l, body, jnp.zeros((depth, LANES), F32))

    def relax(l, v, w, pending=None):
        k = count[0]
        count[0] += 1
        copies = send(k, l, v)
        settle(l, v, pending)

        def body(x0, g, acc):
            parts = [partial(l, v, x0 + j) for j in range(g)]
            d = block_dot(binv_ref[l], jnp.concatenate([p[0] for p in parts], axis=1))
            for j in range(g):
                row = parts[j][1] + d[:, j * LANES:(j + 1) * LANES]
                w[x0 + j + 1] = row
                acc = extract(acc, row, x0 + j, ncol[l])
            return acc

        acc = each_group(l, body, jnp.zeros((depth, LANES), F32))
        for copy in copies:
            copy.wait()
        r, c = nrow[l], ncol[l]
        corr = block_dot(binv_ref[l], jnp.concatenate(halos(k, l), axis=1))
        low, high, beside = (corr[:, j * LANES:(j + 1) * LANES] for j in range(3))
        w[1] = w[1] + low + insert(beside, 0, c)
        w[r] = w[r] + high + insert(beside, r - 1, c)
        acc = acc + beside
        zero = jnp.zeros_like(acc)
        acc = acc + extract(zero, low, 0, c) + extract(zero, high, r - 1, c)
        edge[...] = acc
        return beside

    def settle(l, v, beside):
        if beside is None:
            return
        c = ncol[l]
        for x in range(1, nrow[l] - 1):
            v[x + 1] = v[x + 1] + insert(beside, x, c)

    def residual(l, v, w, pending):
        k = count[0]
        count[0] += 1
        copies = send(k, l, v)
        settle(l, v, pending)

        def body(x0, g, acc):
            for j in range(g):
                w[x0 + j + 1] = partial(l, v, x0 + j)[0]
            return acc

        each_group(l, body)
        for copy in copies:
            copy.wait()
        r, c = nrow[l], ncol[l]
        low, high, beside = halos(k, l)
        w[1] = w[1] + low
        w[r] = w[r] + high
        for x in range(0, r, 2):
            pair = w[x + 1] + w[x + 2] + insert(beside, x, c) + insert(beside, x + 1, c)
            src[l + 1][x // 2] = permute(pair, resm[l])

    def add_coarse(l, v, coarse):
        acc = jnp.zeros((depth, LANES), F32)
        for x in range(nrow[l + 1]):
            fine = permute(coarse[x + 1], prom[l])
            for j in (2 * x, 2 * x + 1):
                row = v[j + 1] + fine
                v[j + 1] = row
                acc = extract(acc, row, j, ncol[l])
        edge[...] = acc

    def cycle(l):
        a, b = va[l], vb[l]
        from_zero(l, a)
        if l == LEVELS - 1:
            p = relax(l, a, b)
            p = relax(l, b, a, p)
            p = relax(l, a, b, p)
            settle(l, b, p)
            return b
        p = relax(l, a, b)
        residual(l, b, a, p)
        add_coarse(l, b, cycle(l + 1))
        p = relax(l, b, a)
        p = relax(l, a, b, p)
        settle(l, b, p)
        return b

    for x in range(rows0):
        src[0][x] = s_in[x] * 16.0
        dia[0][x] = c_in[x] + kz_ref[2]
    for l in range(LEVELS - 1):
        for x in range(nrow[l + 1]):
            dia[l + 1][x] = permute(dia[l][2 * x] + dia[l][2 * x + 1], resm[l])
    pl.semaphore_wait(barrier, 4)
    v = cycle(0)
    for x in range(rows0):
        out_ref[x] = v[x + 1]


def on_device(n_gx, n_gy, right_side, helm_coef, vert_coef, block_inverse, edge_flip):
    nz, rows, cols = right_side.shape
    depth = -(-nz // 8) * 8
    pad = depth - nz
    lay = lambda a: jnp.pad(a.transpose(1, 0, 2), ((0, 0), (0, pad), (0, 0)))
    s, c = lay(right_side), lay(helm_coef)
    kz = jnp.stack([vert_coef[1:], vert_coef[:-1], 4.0 + vert_coef[1:] + vert_coef[:-1]])
    kz = jnp.broadcast_to(jnp.pad(kz, ((0, 0), (0, pad)))[:, :, None], (3, depth, LANES))
    nblk = nz // BLK
    eye = jnp.eye(nblk, dtype=F32)[None, :, None, :, None]
    full = (block_inverse[:, :, :, None, :] * eye).reshape(LEVELS, nz, nz) * 0.0625
    full = jnp.pad(full, ((0, 0), (0, pad), (0, pad)))
    hi = lax.reduce_precision(full, 8, 7)
    binv = jnp.concatenate([hi, hi, full - hi, jnp.zeros((LEVELS, depth, 8), F32)], axis=2).astype(BF)

    tile = lambda r: pltpu.VMEM((r, depth, LANES), F32)
    rl = [rows >> l for l in range(LEVELS)]
    steps = 4 * (LEVELS - 1) + 3
    vm = pl.BlockSpec(memory_space=pltpu.VMEM)
    out = pl.pallas_call(
        functools.partial(kernel, n_gx, n_gy, rows, depth),
        out_shape=jax.ShapeDtypeStruct((rows, depth, LANES), F32),
        in_specs=[pl.BlockSpec(memory_space=pltpu.SMEM), vm, vm, vm, vm],
        out_specs=vm,
        scratch_shapes=[tile(r + 2) for r in rl] * 2 + [tile(r) for r in rl] * 2 + [
            pltpu.VMEM((depth, LANES), F32),
            pltpu.VMEM((steps, 4, depth, LANES), F32),
            pltpu.VMEM((LEVELS, 2, LANES, LANES), BF),
            pltpu.VMEM((LEVELS, 2 * LANES, LANES), BF),
            pltpu.VMEM((LEVELS - 1, LANES, LANES), BF),
            pltpu.VMEM((LEVELS - 1, LANES, LANES), BF),
            pltpu.SemaphoreType.DMA((steps, 4)),
            pltpu.SemaphoreType.DMA((steps, 4)),
        ],
        compiler_params=pltpu.CompilerParams(
            collective_id=0, has_side_effects=True, vmem_limit_bytes=40 * 1024 * 1024),
    )(edge_flip, s, c, kz, binv)
    return out[:, :nz, :].transpose(1, 0, 2)


def solution(mesh):
    placed = (P(None, "gx", "gy"), P(None, "gx", "gy"), P(), P(), P("gx", "gy", None))
    return jax.shard_map(
        functools.partial(on_device, mesh.shape["gx"], mesh.shape["gy"]),
        mesh=mesh, in_specs=placed, out_specs=P(None, "gx", "gy"), check_vma=False)
```

```python
import functools
import jax
import jax.numpy as jnp
from jax import lax
from jax.experimental import pallas as pl
from jax.experimental.pallas import tpu as pltpu
from jax.sharding import PartitionSpec as P

BLK = 14
LEVELS = 4
LANES = 128
MESH = pl.DeviceIdType.MESH
BF = jnp.bfloat16
F32 = jnp.float32


def split2(x):
    hi = x.astype(BF).astype(F32)
    return hi, x - hi


def permute(x, matrix):
    depth = x.shape[0]
    hi, lo = split2(x)
    both = jnp.concatenate([hi, lo], axis=0).astype(BF)
    out = jnp.dot(both, matrix, preferred_element_type=F32)
    return out[:depth] + out[depth:]


FOLD_ROW = (1, 2, 4, 4)
FOLD_END = (2, 4, 4, 4)


def pack(tile, fold):
    width = LANES // fold
    units = tile.shape[0] // 8
    outs = []
    for first in range(0, units, fold):
        acc = tile[8 * first:8 * first + 8]
        for q in range(1, min(fold, units - first)):
            part = tile[8 * (first + q):8 * (first + q) + 8]
            acc = acc + pltpu.roll(part, width * q, 1)
        outs.append(acc)
    return jnp.concatenate(outs, axis=0)


def unpack(packed, matrix, depth, fold):
    wide = permute(packed, matrix)
    parts = []
    for unit in range(depth // 8):
        j, q = divmod(unit, fold)
        parts.append(wide[8 * j:8 * j + 8, LANES * q:LANES * (q + 1)])
    return jnp.concatenate(parts, axis=0)


def block_dot(binv, r):
    hi, lo = split2(r)
    cat = jnp.concatenate([hi, lo, hi, jnp.zeros((8, r.shape[1]), F32)], axis=0).astype(BF)
    return jnp.dot(binv, cat, preferred_element_type=F32)


def kernel(n_gx, n_gy, rows0, depth, flip_ref, s_in, c_in, kz_ref, binv_ref, out_ref,
           stage_s, stage_c, row_send, io_sem,
           va0, va1, va2, va3, vb0, vb1, vb2, vb3, s0, s1, s2, s3, d0, d1, d2, d3,
           edge, held, px, py, resm, prom, send_sem, recv_sem):
    va, vb = (va0, va1, va2, va3), (vb0, vb1, vb2, vb3)
    src, dia = (s0, s1, s2, s3), (d0, d1, d2, d3)
    gx, gy = lax.axis_index("gx"), lax.axis_index("gy")
    peers = (
        (lax.rem(gx + n_gx - 1, n_gx), gy),
        (lax.rem(gx + 1, n_gx), gy),
        (gx, lax.rem(gy + n_gy - 1, n_gy)),
        (gx, lax.rem(gy + 1, n_gy)),
    )
    loads = []
    for x in range(rows0):
        loads.append(pltpu.make_async_copy(s_in.at[:, x, 0, :], stage_s.at[x], io_sem.at[0, x]))
        loads.append(pltpu.make_async_copy(c_in.at[:, x, 0, :], stage_c.at[x], io_sem.at[1, x]))
    for load in loads:
        load.start()
    barrier = pltpu.get_barrier_semaphore()
    for peer in peers:
        pl.semaphore_signal(barrier, inc=1, device_id=peer, device_id_type=MESH)

    nrow = [rows0 >> l for l in range(LEVELS)]
    ncol = [LANES >> l for l in range(LEVELS)]
    lane = lax.broadcasted_iota(jnp.int32, (depth, LANES), 1)
    ki = lax.broadcasted_iota(jnp.int32, (LANES, LANES), 0)
    mi = lax.broadcasted_iota(jnp.int32, (LANES, LANES), 1)
    flips = [flip_ref[0, 0, s] > 0 for s in range(4)]

    def as_matrix(hit, value=1.0):
        return jnp.where(hit, value, 0.0).astype(F32).astype(BF)

    for l in range(LEVELS):
        r, c = nrow[l], ncol[l]
        for side in range(2):
            spot = jnp.where(flips[side], c - 1 - mi, mi)
            for q in range(FOLD_ROW[l]):
                px[l, side, :, LANES * q:LANES * (q + 1)] = as_matrix(
                    (ki == spot + q * (LANES // FOLD_ROW[l])) & (mi < c))
        xm = mi >> 1
        xh = ((mi - c) & (LANES - 1)) >> 1
        for q in range(FOLD_END[l]):
            at = q * (LANES // FOLD_END[l])
            cols = slice(LANES * q, LANES * (q + 1))
            from_low = (2 * jnp.where(flips[2], r - 1 - xm, xm) + c + at) & (LANES - 1)
            py[l, 0:LANES, cols] = as_matrix((ki == from_low) & ((mi & 1) == 1) & (xm < r))
            from_high = (2 * jnp.where(flips[3], r - 1 - xh, xh) + 1 + at) & (LANES - 1)
            py[l, LANES:, cols] = as_matrix((ki == from_high) & ((mi & 1) == 0) & (xh < r))
    for l in range(LEVELS - 1):
        resm[l] = as_matrix(((ki >> 1) == mi) & (mi < ncol[l + 1]), 0.25)
        prom[l] = as_matrix(((mi >> 1) == ki) & (mi < ncol[l]))

    for l in range(LEVELS):
        for buf in (va[l], vb[l]):
            buf[0] = jnp.zeros((depth, LANES), F32)
            buf[nrow[l] + 1] = jnp.zeros((depth, LANES), F32)

    group = [4, 4, 6, 3]

    def each_group(l, body, carry=0):
        g = group[l] if nrow[l] % group[l] == 0 else 1
        trips = nrow[l] // g
        if trips == 1:
            return body(0, g, carry)
        return lax.fori_loop(0, trips, lambda i, acc: body(i * g, g, acc), carry)

    def extract(acc, row, x, c):
        turned = pltpu.roll(row, 2 * x + 1, 1)
        hit = (lane == 2 * x + 1) | (lane == ((2 * x + c) & (LANES - 1)))
        return jnp.where(hit, turned, acc)

    def ends(c):
        return (lane == 0) | (lane == c - 1)

    def insert(tile, x, c):
        return jnp.where(ends(c), pltpu.roll(tile, (LANES - 1) - 2 * x, 1), 0.0)

    def row_size(l):
        return 8 * -(-(depth // 8) // FOLD_ROW[l])

    def end_size(l):
        return 8 * -(-(depth // 8) // FOLD_END[l])

    def put_ends(l, tile):
        edge[0:end_size(l)] = pack(tile, FOLD_END[l])

    def send(k, l, v):
        r = nrow[l]
        if l == 0:
            rows = (v.at[1], v.at[r])
        else:
            size = row_size(l)
            for side, at in ((0, 1), (1, r)):
                row_send[side, 0:size] = pack(jnp.where(lane < ncol[l], v[at], 0.0), FOLD_ROW[l])
            rows = (row_send.at[0, pl.ds(0, size)], row_send.at[1, pl.ds(0, size)])
        size = end_size(l)
        ends_ref = edge.at[pl.ds(0, size)]
        copies = []
        for ref, to, slot in ((rows[0], 0, 1), (rows[1], 1, 0), (ends_ref, 2, 3), (ends_ref, 3, 2)):
            count_z = row_size(l) if to < 2 else size
            copies.append(pltpu.make_async_remote_copy(
                src_ref=ref, dst_ref=held.at[k, slot, pl.ds(0, count_z)], send_sem=send_sem.at[k, slot],
                recv_sem=recv_sem.at[k, slot], device_id=peers[to], device_id_type=MESH))
            copies[-1].start()
        return copies

    up, down = kz_ref[0], kz_ref[1]

    def partial(l, v, x):
        c = ncol[l]
        mid = v[x + 1]
        r = src[l][x] - dia[l][x] * mid + (v[x] + v[x + 2])
        r = r + jnp.where(lane == 0, 0.0, pltpu.roll(mid, 1, 1))
        r = r + jnp.where(lane == c - 1, 0.0, pltpu.roll(mid, LANES - 1, 1))
        r = r + up * pltpu.roll(mid, depth - 1, 0) + down * pltpu.roll(mid, 1, 0)
        return r, mid

    def halos(k, l):
        size = row_size(l)
        low, high = (
            unpack(held[k, side, 0:size], px[l, side, :, 0:LANES * FOLD_ROW[l]], depth, FOLD_ROW[l])
            for side in range(2))
        size = end_size(l)
        both = jnp.concatenate([held[k, 2, 0:size], held[k, 3, 0:size]], axis=1)
        beside = unpack(both, py[l, :, 0:LANES * FOLD_END[l]], depth, FOLD_END[l])
        return low, high, beside

    count = [0]

    def from_zero(l, v):
        def body(x0, g, acc):
            rr = jnp.concatenate([src[l][x0 + j] for j in range(g)], axis=1)
            d = block_dot(binv_ref[l], rr)
            for j in range(g):
                row = d[:, j * LANES:(j + 1) * LANES]
                v[x0 + j + 1] = row
                acc = extract(acc, row, x0 + j, ncol[l])
            return acc
        put_ends(l, each_group(l, body, jnp.zeros((depth, LANES), F32)))

    def relax(l, v, w, pending=None):
        k = count[0]
        count[0] += 1
        copies = send(k, l, v)
        settle(l, v, pending)

        def body(x0, g, acc):
            parts = [partial(l, v, x0 + j) for j in range(g)]
            d = block_dot(binv_ref[l], jnp.concatenate([p[0] for p in parts], axis=1))
            for j in range(g):
                row = parts[j][1] + d[:, j * LANES:(j + 1) * LANES]
                w[x0 + j + 1] = row
                acc = extract(acc, row, x0 + j, ncol[l])
            return acc

        acc = each_group(l, body, jnp.zeros((depth, LANES), F32))
        for copy in copies:
            copy.wait()
        r, c = nrow[l], ncol[l]
        corr = block_dot(binv_ref[l], jnp.concatenate(halos(k, l), axis=1))
        low, high, beside = (corr[:, j * LANES:(j + 1) * LANES] for j in range(3))
        w[1] = w[1] + low + insert(beside, 0, c)
        w[r] = w[r] + high + insert(beside, r - 1, c)
        acc = acc + beside
        zero = jnp.zeros_like(acc)
        acc = acc + extract(zero, low, 0, c) + extract(zero, high, r - 1, c)
        put_ends(l, acc)
        return beside

    def settle(l, v, beside):
        if beside is None:
            return
        c = ncol[l]
        for x in range(1, nrow[l] - 1):
            v[x + 1] = v[x + 1] + insert(beside, x, c)

    def residual(l, v, w, pending):
        k = count[0]
        count[0] += 1
        copies = send(k, l, v)
        settle(l, v, pending)

        def body(x0, g, acc):
            for j in range(g):
                w[x0 + j + 1] = partial(l, v, x0 + j)[0]
            return acc

        each_group(l, body)
        for copy in copies:
            copy.wait()
        r, c = nrow[l], ncol[l]
        low, high, beside = halos(k, l)
        w[1] = w[1] + low
        w[r] = w[r] + high
        for x in range(0, r, 2):
            pair = w[x + 1] + w[x + 2] + insert(beside, x, c) + insert(beside, x + 1, c)
            src[l + 1][x // 2] = permute(pair, resm[l])

    def add_coarse(l, v, coarse):
        acc = jnp.zeros((depth, LANES), F32)
        for x in range(nrow[l + 1]):
            fine = permute(coarse[x + 1], prom[l])
            for j in (2 * x, 2 * x + 1):
                row = v[j + 1] + fine
                v[j + 1] = row
                acc = extract(acc, row, j, ncol[l])
        put_ends(l, acc)

    def cycle(l):
        a, b = va[l], vb[l]
        from_zero(l, a)
        if l == LEVELS - 1:
            p = relax(l, a, b)
            p = relax(l, b, a, p)
            p = relax(l, a, b, p)
            settle(l, b, p)
            return b
        p = relax(l, a, b)
        residual(l, b, a, p)
        add_coarse(l, b, cycle(l + 1))
        p = relax(l, b, a)
        p = relax(l, a, b, p)
        settle(l, b, p)
        return b

    for load in loads:
        load.wait()
    nz = stage_s.shape[1]
    tail = jnp.zeros((depth - nz, LANES), F32)
    for x in range(rows0):
        src[0][x] = jnp.concatenate([stage_s[x] * 16.0, tail], axis=0)
        dia[0][x] = jnp.concatenate([stage_c[x], tail], axis=0) + kz_ref[2]
    for l in range(LEVELS - 1):
        for x in range(nrow[l + 1]):
            dia[l + 1][x] = permute(dia[l][2 * x] + dia[l][2 * x + 1], resm[l])
    pl.semaphore_wait(barrier, 4)
    v = cycle(0)
    stores = []
    for x in range(rows0):
        stage_s[x] = v[x + 1][0:nz]
        stores.append(pltpu.make_async_copy(stage_s.at[x], out_ref.at[:, x, 0, :], io_sem.at[0, x]))
        stores[-1].start()
    for store in stores:
        store.wait()


def on_device(n_gx, n_gy, right_side, helm_coef, vert_coef, block_inverse, edge_flip):
    nz, rows, cols = right_side.shape
    depth = -(-nz // 8) * 8
    pad = depth - nz
    s, c = (a.reshape(nz, rows, 1, cols) for a in (right_side, helm_coef))
    kz = jnp.stack([vert_coef[1:], vert_coef[:-1], 4.0 + vert_coef[1:] + vert_coef[:-1]])
    kz = jnp.broadcast_to(jnp.pad(kz, ((0, 0), (0, pad)))[:, :, None], (3, depth, LANES))
    nblk = nz // BLK
    eye = jnp.eye(nblk, dtype=F32)[None, :, None, :, None]
    full = (block_inverse[:, :, :, None, :] * eye).reshape(LEVELS, nz, nz) * 0.0625
    full = jnp.pad(full, ((0, 0), (0, pad), (0, pad)))
    hi = lax.reduce_precision(full, 8, 7)
    binv = jnp.concatenate([hi, hi, full - hi, jnp.zeros((LEVELS, depth, 8), F32)], axis=2).astype(BF)

    tile = lambda r: pltpu.VMEM((r, depth, LANES), F32)
    rl = [rows >> l for l in range(LEVELS)]
    steps = 4 * (LEVELS - 1) + 3
    hbm = pl.BlockSpec(memory_space=pl.ANY)
    vm = pl.BlockSpec(memory_space=pltpu.VMEM)
    out = pl.pallas_call(
        functools.partial(kernel, n_gx, n_gy, rows, depth),
        out_shape=jax.ShapeDtypeStruct((nz, rows, 1, LANES), F32),
        in_specs=[pl.BlockSpec(memory_space=pltpu.SMEM), hbm, hbm, vm, vm],
        out_specs=hbm,
        scratch_shapes=[
            pltpu.VMEM((rows, nz, LANES), F32),
            pltpu.VMEM((rows, nz, LANES), F32),
            pltpu.VMEM((2, depth, LANES), F32),
            pltpu.SemaphoreType.DMA((2, rows)),
        ] + [tile(r + 2) for r in rl] * 2 + [tile(r) for r in rl] * 2 + [
            pltpu.VMEM((depth, LANES), F32),
            pltpu.VMEM((steps, 4, depth, LANES), F32),
            pltpu.VMEM((LEVELS, 2, LANES, LANES * max(FOLD_ROW)), BF),
            pltpu.VMEM((LEVELS, 2 * LANES, LANES * max(FOLD_END)), BF),
            pltpu.VMEM((LEVELS - 1, LANES, LANES), BF),
            pltpu.VMEM((LEVELS - 1, LANES, LANES), BF),
            pltpu.SemaphoreType.DMA((steps, 4)),
            pltpu.SemaphoreType.DMA((steps, 4)),
        ],
        compiler_params=pltpu.CompilerParams(
            collective_id=0, has_side_effects=True, vmem_limit_bytes=40 * 1024 * 1024),
    )(edge_flip, s, c, kz, binv)
    return out.reshape(nz, rows, cols)


def solution(mesh):
    placed = (P(None, "gx", "gy"), P(None, "gx", "gy"), P(), P(), P("gx", "gy", None))
    return jax.shard_map(
        functools.partial(on_device, mesh.shape["gx"], mesh.shape["gy"]),
        mesh=mesh, in_specs=placed, out_specs=P(None, "gx", "gy"), check_vma=False)
```

```python
import functools
import jax
import jax.numpy as jnp
from jax import lax
from jax.experimental import pallas as pl
from jax.experimental.pallas import tpu as pltpu
from jax.sharding import PartitionSpec as P

BLK = 14
LEVELS = 4
LANES = 128
MESH = pl.DeviceIdType.MESH
BF = jnp.bfloat16
F32 = jnp.float32


def split2(x):
    hi = x.astype(BF).astype(F32)
    return hi, x - hi


def permute(x, matrix):
    depth = x.shape[0]
    hi, lo = split2(x)
    both = jnp.concatenate([hi, lo], axis=0).astype(BF)
    out = jnp.dot(both, matrix, preferred_element_type=F32)
    return out[:depth] + out[depth:]


def permute_many(tiles, matrix):
    depth = tiles[0].shape[0]
    out = permute(jnp.concatenate(tiles, axis=0), matrix)
    return [out[depth * i:depth * (i + 1)] for i in range(len(tiles))]


FOLD_ROW = (1, 2, 4, 4)
FOLD_END = (2, 4, 4, 4)


def pack(tile, fold):
    width = LANES // fold
    units = tile.shape[0] // 8
    outs = []
    for first in range(0, units, fold):
        acc = tile[8 * first:8 * first + 8]
        for q in range(1, min(fold, units - first)):
            part = tile[8 * (first + q):8 * (first + q) + 8]
            acc = acc + pltpu.roll(part, width * q, 1)
        outs.append(acc)
    return jnp.concatenate(outs, axis=0)


def unpack(packed, matrix, depth, fold):
    wide = permute(packed, matrix)
    parts = []
    for unit in range(depth // 8):
        j, q = divmod(unit, fold)
        parts.append(wide[8 * j:8 * j + 8, LANES * q:LANES * (q + 1)])
    return jnp.concatenate(parts, axis=0)


def block_dot(binv, r):
    hi, lo = split2(r)
    cat = jnp.concatenate([hi, lo, hi, jnp.zeros((8, r.shape[1]), F32)], axis=0).astype(BF)
    return jnp.dot(binv, cat, preferred_element_type=F32)


def kernel(n_gx, n_gy, rows0, depth, flip_ref, s_in, c_in, vert_ref, inv_ref, out_ref,
           stage_s, stage_c, row_send, kz_ref, base, binv_ref, io_sem,
           va0, va1, va2, va3, vb0, vb1, vb2, vb3, s0, s1, s2, s3, d0, d1, d2, d3,
           edge, held, px, py, resm, prom, send_sem, recv_sem):
    va, vb = (va0, va1, va2, va3), (vb0, vb1, vb2, vb3)
    src, dia = (s0, s1, s2, s3), (d0, d1, d2, d3)
    gx, gy = lax.axis_index("gx"), lax.axis_index("gy")
    peers = (
        (lax.rem(gx + n_gx - 1, n_gx), gy),
        (lax.rem(gx + 1, n_gx), gy),
        (gx, lax.rem(gy + n_gy - 1, n_gy)),
        (gx, lax.rem(gy + 1, n_gy)),
    )
    load_s = [pltpu.make_async_copy(s_in.at[:, x, 0, :], stage_s.at[x], io_sem.at[0, x])
              for x in range(rows0)]
    load_c = [pltpu.make_async_copy(c_in.at[:, x, 0, :], stage_c.at[x], io_sem.at[1, x])
              for x in range(rows0)]
    for load in load_s + load_c:
        load.start()
    barrier = pltpu.get_barrier_semaphore()
    for peer in peers:
        pl.semaphore_signal(barrier, inc=1, device_id=peer, device_id_type=MESH)

    nrow = [rows0 >> l for l in range(LEVELS)]
    ncol = [LANES >> l for l in range(LEVELS)]
    lane = lax.broadcasted_iota(jnp.int32, (depth, LANES), 1)
    ki = lax.broadcasted_iota(jnp.int32, (LANES, LANES), 0)
    mi = lax.broadcasted_iota(jnp.int32, (LANES, LANES), 1)
    level_z = lax.broadcasted_iota(jnp.int32, (depth, LANES), 0)
    nz = stage_s.shape[1]
    coef = jnp.broadcast_to(vert_ref[...], (depth, LANES))

    def down_lanes(shift):
        hit = (lane == level_z + shift) & (level_z < nz)
        return jnp.broadcast_to(jnp.sum(jnp.where(hit, coef, 0.0), axis=1, keepdims=True), (depth, LANES))

    up, down = down_lanes(1), down_lanes(0)
    kz_ref[0] = up
    kz_ref[1] = down
    kz_ref[2] = jnp.where(level_z < nz, 4.0 + up + down, 0.0)
    nblk, blk = inv_ref.shape[0], inv_ref.shape[1]
    for l in range(LEVELS):
        base[l] = jnp.zeros((depth, LANES), F32)
        for k in range(nblk):
            base[l, blk * k:blk * (k + 1), 0:blk] = inv_ref[k, :, l, :] * 0.0625
        block = base[l]
        full = block
        for k in range(1, nblk):
            full = jnp.where(level_z >= blk * k, pltpu.roll(block, blk * k, 1), full)
        hi, lo = split2(full)
        turned = pltpu.roll(hi, depth, 1)
        first = jnp.where(lane < depth, hi, turned)
        second = jnp.where(lane < 2 * depth - LANES, turned, pltpu.roll(lo, 2 * depth - LANES, 1))
        binv_ref[l] = jnp.concatenate([first, second], axis=1).astype(BF)
    flips = [flip_ref[0, 0, s] > 0 for s in range(4)]

    def as_matrix(hit, value=1.0):
        return jnp.where(hit, value, 0.0).astype(F32).astype(BF)

    for l in range(LEVELS):
        r, c = nrow[l], ncol[l]
        for side in range(2):
            spot = jnp.where(flips[side], c - 1 - mi, mi)
            for q in range(FOLD_ROW[l]):
                px[l, side, :, LANES * q:LANES * (q + 1)] = as_matrix(
                    (ki == spot + q * (LANES // FOLD_ROW[l])) & (mi < c))
        xm = mi >> 1
        xh = ((mi - c) & (LANES - 1)) >> 1
        for q in range(FOLD_END[l]):
            at = q * (LANES // FOLD_END[l])
            cols = slice(LANES * q, LANES * (q + 1))
            from_low = (2 * jnp.where(flips[2], r - 1 - xm, xm) + c + at) & (LANES - 1)
            py[l, 0:LANES, cols] = as_matrix((ki == from_low) & ((mi & 1) == 1) & (xm < r))
            from_high = (2 * jnp.where(flips[3], r - 1 - xh, xh) + 1 + at) & (LANES - 1)
            py[l, LANES:, cols] = as_matrix((ki == from_high) & ((mi & 1) == 0) & (xh < r))
    for l in range(LEVELS - 1):
        resm[l] = as_matrix(((ki >> 1) == mi) & (mi < ncol[l + 1]), 0.25)
        prom[l] = as_matrix(((mi >> 1) == ki) & (mi < ncol[l]))

    for l in range(LEVELS):
        for buf in (va[l], vb[l]):
            buf[0] = jnp.zeros((depth, LANES), F32)
            buf[nrow[l] + 1] = jnp.zeros((depth, LANES), F32)

    group = [4, 4, 3, 3]
    per_step = [8, 12, 6, 3]

    def each_group(l, body, carry=0):
        g = group[l] if nrow[l] % group[l] == 0 else 1
        step = per_step[l] if nrow[l] % per_step[l] == 0 else g

        def run(x0, acc):
            for off in range(0, step, g):
                acc = body(x0 + off, g, acc)
            return acc

        if step == nrow[l]:
            return run(0, carry)
        return lax.fori_loop(0, nrow[l] // step, lambda i, acc: run(i * step, acc), carry)

    def extract(acc, row, x, c):
        turned = pltpu.roll(row, 2 * x + 1, 1)
        hit = (lane == 2 * x + 1) | (lane == ((2 * x + c) & (LANES - 1)))
        return jnp.where(hit, turned, acc)

    def ends(c):
        return (lane == 0) | (lane == c - 1)

    def insert(tile, x, c):
        return jnp.where(ends(c), pltpu.roll(tile, (LANES - 1) - 2 * x, 1), 0.0)

    def row_size(l):
        return 8 * -(-(depth // 8) // FOLD_ROW[l])

    def end_size(l):
        return 8 * -(-(depth // 8) // FOLD_END[l])

    def put_ends(l, tile):
        edge[0:end_size(l)] = pack(tile, FOLD_END[l])

    def send(k, l, v):
        r = nrow[l]
        if l == 0:
            rows = (v.at[1], v.at[r])
        else:
            size = row_size(l)
            for side, at in ((0, 1), (1, r)):
                row_send[side, 0:size] = pack(jnp.where(lane < ncol[l], v[at], 0.0), FOLD_ROW[l])
            rows = (row_send.at[0, pl.ds(0, size)], row_send.at[1, pl.ds(0, size)])
        size = end_size(l)
        ends_ref = edge.at[pl.ds(0, size)]
        copies = []
        for ref, to, slot in ((rows[0], 0, 1), (rows[1], 1, 0), (ends_ref, 2, 3), (ends_ref, 3, 2)):
            count_z = row_size(l) if to < 2 else size
            copies.append(pltpu.make_async_remote_copy(
                src_ref=ref, dst_ref=held.at[k, slot, pl.ds(0, count_z)], send_sem=send_sem.at[k, slot],
                recv_sem=recv_sem.at[k, slot], device_id=peers[to], device_id_type=MESH))
            copies[-1].start()
        return copies

    def partial(l, v, x):
        c = ncol[l]
        mid = v[x + 1]
        r = src[l][x] - dia[l][x] * mid + (v[x] + v[x + 2])
        r = r + jnp.where(lane == 0, 0.0, pltpu.roll(mid, 1, 1))
        r = r + jnp.where(lane == c - 1, 0.0, pltpu.roll(mid, LANES - 1, 1))
        r = r + kz_ref[0] * pltpu.roll(mid, depth - 1, 0) + kz_ref[1] * pltpu.roll(mid, 1, 0)
        return r, mid

    def halos(k, l):
        size = row_size(l)
        low, high = (
            unpack(held[k, side, 0:size], px[l, side, :, 0:LANES * FOLD_ROW[l]], depth, FOLD_ROW[l])
            for side in range(2))
        size = end_size(l)
        both = jnp.concatenate([held[k, 2, 0:size], held[k, 3, 0:size]], axis=1)
        beside = unpack(both, py[l, :, 0:LANES * FOLD_END[l]], depth, FOLD_END[l])
        return low, high, beside

    count = [0]

    tail = jnp.zeros((depth - nz, LANES), F32)

    def first_field(v):
        acc = jnp.zeros((depth, LANES), F32)
        g = 4 if rows0 % 4 == 0 else 1
        for x0 in range(0, rows0, g):
            rows = []
            for x in range(x0, x0 + g):
                load_s[x].wait()
                rows.append(jnp.concatenate([stage_s[x] * 16.0, tail], axis=0))
                src[0][x] = rows[-1]
            d = block_dot(binv_ref[0, :, 0:3 * depth + 8], jnp.concatenate(rows, axis=1))
            for j in range(g):
                row = d[:, j * LANES:(j + 1) * LANES]
                v[x0 + j + 1] = row
                acc = extract(acc, row, x0 + j, ncol[0])
        put_ends(0, acc)

    def take_coef():
        for x in range(rows0):
            load_c[x].wait()
            dia[0][x] = jnp.concatenate([stage_c[x], tail], axis=0) + kz_ref[2]

    def coarse_coef():
        for l in range(LEVELS - 1):
            pairs = [dia[l][2 * x] + dia[l][2 * x + 1] for x in range(nrow[l + 1])]
            for x, row in enumerate(permute_many(pairs, resm[l])):
                dia[l + 1][x] = row

    def from_zero(l, v):
        def body(x0, g, acc):
            rr = jnp.concatenate([src[l][x0 + j] for j in range(g)], axis=1)
            d = block_dot(binv_ref[l, :, 0:3 * depth + 8], rr)
            for j in range(g):
                row = d[:, j * LANES:(j + 1) * LANES]
                v[x0 + j + 1] = row
                acc = extract(acc, row, x0 + j, ncol[l])
            return acc
        put_ends(l, each_group(l, body, jnp.zeros((depth, LANES), F32)))

    def relax(l, v, w, pending=None, start=False):
        k = count[0]
        count[0] += 1
        copies = send(k, l, v)
        settle(l, v, pending)
        if start:
            take_coef()

        def body(x0, g, acc):
            parts = [partial(l, v, x0 + j) for j in range(g)]
            d = block_dot(binv_ref[l, :, 0:3 * depth + 8], jnp.concatenate([p[0] for p in parts], axis=1))
            for j in range(g):
                row = parts[j][1] + d[:, j * LANES:(j + 1) * LANES]
                w[x0 + j + 1] = row
                acc = extract(acc, row, x0 + j, ncol[l])
            return acc

        acc = each_group(l, body, jnp.zeros((depth, LANES), F32))
        if start:
            coarse_coef()
        for copy in copies:
            copy.wait()
        r, c = nrow[l], ncol[l]
        corr = block_dot(binv_ref[l, :, 0:3 * depth + 8], jnp.concatenate(halos(k, l), axis=1))
        low, high, beside = (corr[:, j * LANES:(j + 1) * LANES] for j in range(3))
        w[1] = w[1] + low + insert(beside, 0, c)
        w[r] = w[r] + high + insert(beside, r - 1, c)
        acc = acc + beside
        zero = jnp.zeros_like(acc)
        acc = acc + extract(zero, low, 0, c) + extract(zero, high, r - 1, c)
        put_ends(l, acc)
        return beside

    def settle(l, v, beside):
        if beside is None:
            return
        c = ncol[l]
        for x in range(1, nrow[l] - 1):
            v[x + 1] = v[x + 1] + insert(beside, x, c)

    def residual(l, v, w, pending):
        k = count[0]
        count[0] += 1
        copies = send(k, l, v)
        settle(l, v, pending)

        def body(x0, g, acc):
            for j in range(g):
                w[x0 + j + 1] = partial(l, v, x0 + j)[0]
            return acc

        each_group(l, body)
        for copy in copies:
            copy.wait()
        r, c = nrow[l], ncol[l]
        low, high, beside = halos(k, l)
        w[1] = w[1] + low
        w[r] = w[r] + high
        pairs = [w[x + 1] + w[x + 2] + insert(beside, x, c) + insert(beside, x + 1, c)
                 for x in range(0, r, 2)]
        for x, row in enumerate(permute_many(pairs, resm[l])):
            src[l + 1][x] = row

    def add_coarse(l, v, coarse):
        acc = jnp.zeros((depth, LANES), F32)
        spread = permute_many([coarse[x + 1] for x in range(nrow[l + 1])], prom[l])
        for x, fine in enumerate(spread):
            for j in (2 * x, 2 * x + 1):
                row = v[j + 1] + fine
                v[j + 1] = row
                acc = extract(acc, row, j, ncol[l])
        put_ends(l, acc)

    def cycle(l):
        a, b = va[l], vb[l]
        if l == 0:
            first_field(a)
            pl.semaphore_wait(barrier, 4)
        else:
            from_zero(l, a)
        if l == LEVELS - 1:
            p = relax(l, a, b)
            p = relax(l, b, a, p)
            p = relax(l, a, b, p)
            settle(l, b, p)
            return b
        p = relax(l, a, b, start=l == 0)
        residual(l, b, a, p)
        add_coarse(l, b, cycle(l + 1))
        p = relax(l, b, a)
        p = relax(l, a, b, p)
        settle(l, b, p)
        return b

    v = cycle(0)
    stores = []
    for x in range(rows0):
        stage_s[x] = v[x + 1][0:nz]
        stores.append(pltpu.make_async_copy(stage_s.at[x], out_ref.at[:, x, 0, :], io_sem.at[0, x]))
        stores[-1].start()
    for store in stores:
        store.wait()


def on_device(n_gx, n_gy, right_side, helm_coef, vert_coef, block_inverse, edge_flip):
    nz, rows, cols = right_side.shape
    depth = -(-nz // 8) * 8
    s, c = (a.reshape(nz, rows, 1, cols) for a in (right_side, helm_coef))
    vert = jnp.pad(vert_coef, (0, LANES - nz - 1)).reshape(1, LANES)
    inv = block_inverse.transpose(1, 2, 0, 3)

    tile = lambda r: pltpu.VMEM((r, depth, LANES), F32)
    rl = [rows >> l for l in range(LEVELS)]
    steps = 4 * (LEVELS - 1) + 3
    hbm = pl.BlockSpec(memory_space=pl.ANY)
    vm = pl.BlockSpec(memory_space=pltpu.VMEM)
    out = pl.pallas_call(
        functools.partial(kernel, n_gx, n_gy, rows, depth),
        out_shape=jax.ShapeDtypeStruct((nz, rows, 1, LANES), F32),
        in_specs=[pl.BlockSpec(memory_space=pltpu.SMEM), hbm, hbm, vm, vm],
        out_specs=hbm,
        scratch_shapes=[
            pltpu.VMEM((rows, nz, LANES), F32),
            pltpu.VMEM((rows, nz, LANES), F32),
            pltpu.VMEM((2, depth, LANES), F32),
            pltpu.VMEM((3, depth, LANES), F32),
            pltpu.VMEM((LEVELS, depth, LANES), F32),
            pltpu.VMEM((LEVELS, depth, 2 * LANES), BF),
            pltpu.SemaphoreType.DMA((2, rows)),
        ] + [tile(r + 2) for r in rl] * 2 + [tile(r) for r in rl] * 2 + [
            pltpu.VMEM((depth, LANES), F32),
            pltpu.VMEM((steps, 4, depth, LANES), F32),
            pltpu.VMEM((LEVELS, 2, LANES, LANES * max(FOLD_ROW)), BF),
            pltpu.VMEM((LEVELS, 2 * LANES, LANES * max(FOLD_END)), BF),
            pltpu.VMEM((LEVELS - 1, LANES, LANES), BF),
            pltpu.VMEM((LEVELS - 1, LANES, LANES), BF),
            pltpu.SemaphoreType.DMA((steps, 4)),
            pltpu.SemaphoreType.DMA((steps, 4)),
        ],
        compiler_params=pltpu.CompilerParams(
            collective_id=0, has_side_effects=True, vmem_limit_bytes=60 * 1024 * 1024),
    )(edge_flip, s, c, vert, inv)
    return out.reshape(nz, rows, cols)


def solution(mesh):
    placed = (P(None, "gx", "gy"), P(None, "gx", "gy"), P(), P(), P("gx", "gy", None))
    return jax.shard_map(
        functools.partial(on_device, mesh.shape["gx"], mesh.shape["gy"]),
        mesh=mesh, in_specs=placed, out_specs=P(None, "gx", "gy"), check_vma=False)
```

```python
import functools
import jax
import jax.numpy as jnp
from jax import lax
from jax.experimental import pallas as pl
from jax.experimental.pallas import tpu as pltpu
from jax.sharding import PartitionSpec as P

BLK = 14
LEVELS = 4
LANES = 128
MESH = pl.DeviceIdType.MESH
BF = jnp.bfloat16
F32 = jnp.float32


def split2(x):
    hi = x.astype(BF).astype(F32)
    return hi, x - hi


def take(tile, spot):
    return jnp.take_along_axis(tile, spot, axis=1, mode="promise_in_bounds")


FOLD_ROW = (1, 2, 4, 4)
FOLD_END = (2, 4, 4, 4)


def pack(tile, fold):
    width = LANES // fold
    units = tile.shape[0] // 8
    outs = []
    for first in range(0, units, fold):
        acc = tile[8 * first:8 * first + 8]
        for q in range(1, min(fold, units - first)):
            part = tile[8 * (first + q):8 * (first + q) + 8]
            acc = acc + pltpu.roll(part, width * q, 1)
        outs.append(acc)
    return jnp.concatenate(outs, axis=0)


def unpack(packed, spot, keep, depth, fold):
    parts = []
    for unit in range(depth // 8):
        j, q = divmod(unit, fold)
        at = (spot + q * (LANES // fold)) & (LANES - 1)
        parts.append(jnp.where(keep, take(packed[8 * j:8 * j + 8], at), 0.0))
    return jnp.concatenate(parts, axis=0)


def block_dot(binv, r):
    hi, lo = split2(r)
    cat = jnp.concatenate([hi, lo, hi, jnp.zeros((8, r.shape[1]), F32)], axis=0).astype(BF)
    return jnp.dot(binv, cat, preferred_element_type=F32)


def kernel(n_gx, n_gy, rows0, depth, flip_ref, s_in, c_in, vert_ref, inv_ref, out_ref,
           stage_s, stage_c, row_send, kz_ref, base, binv_ref, io_sem,
           va0, va1, va2, va3, vb0, vb1, vb2, vb3, s0, s1, s2, s3, d0, d1, d2, d3,
           edge, held, send_sem, recv_sem):
    va, vb = (va0, va1, va2, va3), (vb0, vb1, vb2, vb3)
    src, dia = (s0, s1, s2, s3), (d0, d1, d2, d3)
    gx, gy = lax.axis_index("gx"), lax.axis_index("gy")
    peers = (
        (lax.rem(gx + n_gx - 1, n_gx), gy),
        (lax.rem(gx + 1, n_gx), gy),
        (gx, lax.rem(gy + n_gy - 1, n_gy)),
        (gx, lax.rem(gy + 1, n_gy)),
    )
    load_s = [pltpu.make_async_copy(s_in.at[:, x, 0, :], stage_s.at[x], io_sem.at[0, x])
              for x in range(rows0)]
    load_c = [pltpu.make_async_copy(c_in.at[:, x, 0, :], stage_c.at[x], io_sem.at[1, x])
              for x in range(rows0)]
    for load in load_s + load_c:
        load.start()
    barrier = pltpu.get_barrier_semaphore()
    for peer in peers:
        pl.semaphore_signal(barrier, inc=1, device_id=peer, device_id_type=MESH)

    nrow = [rows0 >> l for l in range(LEVELS)]
    ncol = [LANES >> l for l in range(LEVELS)]
    lane = lax.broadcasted_iota(jnp.int32, (depth, LANES), 1)
    level_z = lax.broadcasted_iota(jnp.int32, (depth, LANES), 0)
    nz = stage_s.shape[1]
    coef = jnp.concatenate([vert_ref[...], jnp.zeros((1, LANES - nz - 1), F32)], axis=1)
    coef = jnp.broadcast_to(coef, (depth, LANES))

    def down_lanes(shift):
        hit = (lane == level_z + shift) & (level_z < nz)
        return jnp.broadcast_to(jnp.sum(jnp.where(hit, coef, 0.0), axis=1, keepdims=True), (depth, LANES))

    up, down = down_lanes(1), down_lanes(0)
    kz_ref[0] = up
    kz_ref[1] = down
    kz_ref[2] = jnp.where(level_z < nz, 4.0 + up + down, 0.0)
    nblk, blk = inv_ref.shape[0], inv_ref.shape[1]
    for l in range(LEVELS):
        base[l] = jnp.zeros((depth, LANES), F32)
        for k in range(nblk):
            base[l, blk * k:blk * (k + 1), 0:blk] = inv_ref[k, :, l, :] * 0.0625
        block = base[l]
        full = block
        for k in range(1, nblk):
            full = jnp.where(level_z >= blk * k, pltpu.roll(block, blk * k, 1), full)
        hi, lo = split2(full)
        turned = pltpu.roll(hi, depth, 1)
        first = jnp.where(lane < depth, hi, turned)
        second = jnp.where(lane < 2 * depth - LANES, turned, pltpu.roll(lo, 2 * depth - LANES, 1))
        binv_ref[l] = jnp.concatenate([first, second], axis=1).astype(BF)
    flips = [flip_ref[0, 0, s] > 0 for s in range(4)]

    lane8 = lax.broadcasted_iota(jnp.int32, (8, LANES), 1)

    def restrict(row, l):
        both = row + pltpu.roll(row, LANES - 1, 1)
        return jnp.where(lane < ncol[l + 1], take(both, (2 * lane) & (LANES - 1)) * 0.25, 0.0)

    for l in range(LEVELS):
        for buf in (va[l], vb[l]):
            buf[0] = jnp.zeros((depth, LANES), F32)
            buf[nrow[l] + 1] = jnp.zeros((depth, LANES), F32)

    group = [4, 4, 3, 3]
    per_step = [8, 12, 6, 3]

    def each_group(l, body, carry=0):
        g = group[l] if nrow[l] % group[l] == 0 else 1
        step = per_step[l] if nrow[l] % per_step[l] == 0 else g

        def run(x0, acc):
            for off in range(0, step, g):
                acc = body(x0 + off, g, acc)
            return acc

        if step == nrow[l]:
            return run(0, carry)
        return lax.fori_loop(0, nrow[l] // step, lambda i, acc: run(i * step, acc), carry)

    def extract(acc, row, x, c):
        turned = pltpu.roll(row, 2 * x + 1, 1)
        hit = (lane == 2 * x + 1) | (lane == ((2 * x + c) & (LANES - 1)))
        return jnp.where(hit, turned, acc)

    def ends(c):
        return (lane == 0) | (lane == c - 1)

    def insert(tile, x, c):
        return jnp.where(ends(c), pltpu.roll(tile, (LANES - 1) - 2 * x, 1), 0.0)

    def row_size(l):
        return 8 * -(-(depth // 8) // FOLD_ROW[l])

    def end_size(l):
        return 8 * -(-(depth // 8) // FOLD_END[l])

    def put_ends(l, tile):
        edge[0:end_size(l)] = pack(tile, FOLD_END[l])

    def send(k, l, v):
        r = nrow[l]
        if l == 0:
            rows = (v.at[1], v.at[r])
        else:
            size = row_size(l)
            for side, at in ((0, 1), (1, r)):
                row_send[side, 0:size] = pack(jnp.where(lane < ncol[l], v[at], 0.0), FOLD_ROW[l])
            rows = (row_send.at[0, pl.ds(0, size)], row_send.at[1, pl.ds(0, size)])
        size = end_size(l)
        ends_ref = edge.at[pl.ds(0, size)]
        copies = []
        for ref, to, slot in ((rows[0], 0, 1), (rows[1], 1, 0), (ends_ref, 2, 3), (ends_ref, 3, 2)):
            count_z = row_size(l) if to < 2 else size
            copies.append(pltpu.make_async_remote_copy(
                src_ref=ref, dst_ref=held.at[k, slot, pl.ds(0, count_z)], send_sem=send_sem.at[k, slot],
                recv_sem=recv_sem.at[k, slot], device_id=peers[to], device_id_type=MESH))
            copies[-1].start()
        return copies

    def partial(l, v, x):
        c = ncol[l]
        mid = v[x + 1]
        r = src[l][x] - dia[l][x] * mid + (v[x] + v[x + 2])
        r = r + jnp.where(lane == 0, 0.0, pltpu.roll(mid, 1, 1))
        r = r + jnp.where(lane == c - 1, 0.0, pltpu.roll(mid, LANES - 1, 1))
        r = r + kz_ref[0] * pltpu.roll(mid, depth - 1, 0) + kz_ref[1] * pltpu.roll(mid, 1, 0)
        return r, mid

    def halos(k, l):
        r, c = nrow[l], ncol[l]
        size = row_size(l)
        low, high = (
            unpack(held[k, side, 0:size], jnp.where(flips[side], c - 1 - lane8, lane8), lane8 < c,
                   depth, FOLD_ROW[l])
            for side in range(2))
        size = end_size(l)
        odd = (lane8 & 1) == 1
        xm = lane8 >> 1
        xh = ((lane8 - c) & (LANES - 1)) >> 1
        from_low = 2 * jnp.where(flips[2], r - 1 - xm, xm) + c
        from_high = 2 * jnp.where(flips[3], r - 1 - xh, xh) + 1
        keep = jnp.where(odd, xm, xh) < r
        both = jnp.where((lane[0:size] & 1) == 1, held[k, 3, 0:size], held[k, 2, 0:size])
        beside = unpack(both, jnp.where(odd, from_low, from_high), keep, depth, FOLD_END[l])
        return low, high, beside

    count = [0]

    tail = jnp.zeros((depth - nz, LANES), F32)

    def first_field(v):
        acc = jnp.zeros((depth, LANES), F32)
        g = 4 if rows0 % 4 == 0 else 1
        for x0 in range(0, rows0, g):
            rows = []
            for x in range(x0, x0 + g):
                load_s[x].wait()
                rows.append(jnp.concatenate([stage_s[x] * 16.0, tail], axis=0))
                src[0][x] = rows[-1]
            d = block_dot(binv_ref[0, :, 0:3 * depth + 8], jnp.concatenate(rows, axis=1))
            for j in range(g):
                row = d[:, j * LANES:(j + 1) * LANES]
                v[x0 + j + 1] = row
                acc = extract(acc, row, x0 + j, ncol[0])
        put_ends(0, acc)

    def take_coef():
        for x in range(rows0):
            load_c[x].wait()
            dia[0][x] = jnp.concatenate([stage_c[x], tail], axis=0) + kz_ref[2]

    def coarse_coef():
        for l in range(LEVELS - 1):
            for x in range(nrow[l + 1]):
                dia[l + 1][x] = restrict(dia[l][2 * x] + dia[l][2 * x + 1], l)

    def from_zero(l, v):
        def body(x0, g, acc):
            rr = jnp.concatenate([src[l][x0 + j] for j in range(g)], axis=1)
            d = block_dot(binv_ref[l, :, 0:3 * depth + 8], rr)
            for j in range(g):
                row = d[:, j * LANES:(j + 1) * LANES]
                v[x0 + j + 1] = row
                acc = extract(acc, row, x0 + j, ncol[l])
            return acc
        put_ends(l, each_group(l, body, jnp.zeros((depth, LANES), F32)))

    def relax(l, v, w, pending=None, start=False):
        k = count[0]
        count[0] += 1
        copies = send(k, l, v)
        settle(l, v, pending)
        if start:
            take_coef()

        def body(x0, g, acc):
            parts = [partial(l, v, x0 + j) for j in range(g)]
            d = block_dot(binv_ref[l, :, 0:3 * depth + 8], jnp.concatenate([p[0] for p in parts], axis=1))
            for j in range(g):
                row = parts[j][1] + d[:, j * LANES:(j + 1) * LANES]
                w[x0 + j + 1] = row
                acc = extract(acc, row, x0 + j, ncol[l])
            return acc

        acc = each_group(l, body, jnp.zeros((depth, LANES), F32))
        if start:
            coarse_coef()
        for copy in copies:
            copy.wait()
        r, c = nrow[l], ncol[l]
        corr = block_dot(binv_ref[l, :, 0:3 * depth + 8], jnp.concatenate(halos(k, l), axis=1))
        low, high, beside = (corr[:, j * LANES:(j + 1) * LANES] for j in range(3))
        w[1] = w[1] + low + insert(beside, 0, c)
        w[r] = w[r] + high + insert(beside, r - 1, c)
        acc = acc + beside
        zero = jnp.zeros_like(acc)
        acc = acc + extract(zero, low, 0, c) + extract(zero, high, r - 1, c)
        put_ends(l, acc)
        return beside

    def settle(l, v, beside):
        if beside is None:
            return
        c = ncol[l]
        for x in range(1, nrow[l] - 1):
            v[x + 1] = v[x + 1] + insert(beside, x, c)

    def residual(l, v, w, pending):
        k = count[0]
        count[0] += 1
        copies = send(k, l, v)
        settle(l, v, pending)

        def body(x0, g, acc):
            for j in range(g):
                w[x0 + j + 1] = partial(l, v, x0 + j)[0]
            return acc

        each_group(l, body)
        for copy in copies:
            copy.wait()
        r, c = nrow[l], ncol[l]
        low, high, beside = halos(k, l)
        w[1] = w[1] + low
        w[r] = w[r] + high
        for x in range(0, r, 2):
            pair = w[x + 1] + w[x + 2] + insert(beside, x, c) + insert(beside, x + 1, c)
            src[l + 1][x // 2] = restrict(pair, l)

    def add_coarse(l, v, coarse):
        acc = jnp.zeros((depth, LANES), F32)
        for x in range(nrow[l + 1]):
            fine = take(coarse[x + 1], lane >> 1)
            for j in (2 * x, 2 * x + 1):
                row = v[j + 1] + fine
                v[j + 1] = row
                acc = extract(acc, row, j, ncol[l])
        put_ends(l, acc)

    def cycle(l):
        a, b = va[l], vb[l]
        if l == 0:
            first_field(a)
            pl.semaphore_wait(barrier, 4)
        else:
            from_zero(l, a)
        if l == LEVELS - 1:
            p = relax(l, a, b)
            p = relax(l, b, a, p)
            p = relax(l, a, b, p)
            settle(l, b, p)
            return b
        p = relax(l, a, b, start=l == 0)
        residual(l, b, a, p)
        add_coarse(l, b, cycle(l + 1))
        p = relax(l, b, a)
        p = relax(l, a, b, p)
        settle(l, b, p)
        return b

    v = cycle(0)
    stores = []
    for x in range(rows0):
        stage_s[x] = v[x + 1][0:nz]
        stores.append(pltpu.make_async_copy(stage_s.at[x], out_ref.at[:, x, 0, :], io_sem.at[0, x]))
        stores[-1].start()
    for store in stores:
        store.wait()


def on_device(n_gx, n_gy, right_side, helm_coef, vert_coef, block_inverse, edge_flip):
    nz, rows, cols = right_side.shape
    depth = -(-nz // 8) * 8
    s, c = (a.reshape(nz, rows, 1, cols) for a in (right_side, helm_coef))
    vert = vert_coef.reshape(1, nz + 1)
    inv = block_inverse.transpose(1, 2, 0, 3)

    tile = lambda r: pltpu.VMEM((r, depth, LANES), F32)
    rl = [rows >> l for l in range(LEVELS)]
    steps = 4 * (LEVELS - 1) + 3
    hbm = pl.BlockSpec(memory_space=pl.ANY)
    far = pl.BlockSpec(memory_space=pltpu.HBM)
    vm = pl.BlockSpec(memory_space=pltpu.VMEM)
    out = pl.pallas_call(
        functools.partial(kernel, n_gx, n_gy, rows, depth),
        out_shape=jax.ShapeDtypeStruct((nz, rows, 1, LANES), F32),
        in_specs=[pl.BlockSpec(memory_space=pltpu.SMEM), far, far, vm, vm],
        out_specs=hbm,
        scratch_shapes=[
            pltpu.VMEM((rows, nz, LANES), F32),
            pltpu.VMEM((rows, nz, LANES), F32),
            pltpu.VMEM((2, depth, LANES), F32),
            pltpu.VMEM((3, depth, LANES), F32),
            pltpu.VMEM((LEVELS, depth, LANES), F32),
            pltpu.VMEM((LEVELS, depth, 2 * LANES), BF),
            pltpu.SemaphoreType.DMA((2, rows)),
        ] + [tile(r + 2) for r in rl] * 2 + [tile(r) for r in rl] * 2 + [
            pltpu.VMEM((depth, LANES), F32),
            pltpu.VMEM((steps, 4, depth, LANES), F32),
            pltpu.SemaphoreType.DMA((steps, 4)),
            pltpu.SemaphoreType.DMA((steps, 4)),
        ],
        compiler_params=pltpu.CompilerParams(
            collective_id=0, has_side_effects=True, vmem_limit_bytes=40 * 1024 * 1024),
    )(edge_flip, s, c, vert, inv)
    return out.reshape(nz, rows, cols)


def solution(mesh):
    placed = (P(None, "gx", "gy"), P(None, "gx", "gy"), P(), P(), P("gx", "gy", None))
    return jax.shard_map(
        functools.partial(on_device, mesh.shape["gx"], mesh.shape["gy"]),
        mesh=mesh, in_specs=placed, out_specs=P(None, "gx", "gy"), check_vma=False)
```

```python
import functools
import jax
import jax.numpy as jnp
from jax import lax
from jax.experimental import pallas as pl
from jax.experimental.pallas import tpu as pltpu
from jax.sharding import PartitionSpec as P

BLK = 14
LEVELS = 4
LANES = 128
MESH = pl.DeviceIdType.MESH
BF = jnp.bfloat16
F32 = jnp.float32


def split2(x):
    hi = x.astype(BF).astype(F32)
    return hi, x - hi


def take(tile, spot):
    return jnp.take_along_axis(tile, spot, axis=1, mode="promise_in_bounds")


FOLD_ROW = (1, 2, 4, 4)
FOLD_END = (2, 4, 4, 4)


def pack(tile, fold):
    width = LANES // fold
    units = tile.shape[0] // 8
    outs = []
    for first in range(0, units, fold):
        acc = tile[8 * first:8 * first + 8]
        for q in range(1, min(fold, units - first)):
            part = tile[8 * (first + q):8 * (first + q) + 8]
            acc = acc + pltpu.roll(part, width * q, 1)
        outs.append(acc)
    return jnp.concatenate(outs, axis=0)


def unpack(packed, spot, keep, depth, fold):
    parts = []
    for unit in range(depth // 8):
        j, q = divmod(unit, fold)
        at = (spot + q * (LANES // fold)) & (LANES - 1)
        parts.append(jnp.where(keep, take(packed[8 * j:8 * j + 8], at), 0.0))
    return jnp.concatenate(parts, axis=0)


def block_dot(binv, r):
    hi, lo = split2(r)
    cat = jnp.concatenate([hi, lo, hi, jnp.zeros((8, r.shape[1]), F32)], axis=0).astype(BF)
    return jnp.dot(binv, cat, preferred_element_type=F32)


def kernel(n_gx, n_gy, rows0, depth, flip_ref, s_in, c_in, vert_ref, inv_ref, out_ref,
           stage_s, stage_c, row_send, kz_ref, base, binv_ref, io_sem,
           va0, va1, va2, va3, vb0, vb1, vb2, vb3, s0, s1, s2, s3, d0, d1, d2, d3,
           edge, held, send_sem, recv_sem):
    va, vb = (va0, va1, va2, va3), (vb0, vb1, vb2, vb3)
    src, dia = (s0, s1, s2, s3), (d0, d1, d2, d3)
    gx, gy = lax.axis_index("gx"), lax.axis_index("gy")
    peers = (
        (lax.rem(gx + n_gx - 1, n_gx), gy),
        (lax.rem(gx + 1, n_gx), gy),
        (gx, lax.rem(gy + n_gy - 1, n_gy)),
        (gx, lax.rem(gy + 1, n_gy)),
    )
    load_s = [pltpu.make_async_copy(s_in.at[:, x, 0, :], stage_s.at[x], io_sem.at[0, x])
              for x in range(rows0)]
    load_c = [pltpu.make_async_copy(c_in.at[:, x, 0, :], stage_c.at[x], io_sem.at[1, x])
              for x in range(rows0)]
    for load in load_s + load_c:
        load.start()
    barrier = pltpu.get_barrier_semaphore()
    for peer in peers:
        pl.semaphore_signal(barrier, inc=1, device_id=peer, device_id_type=MESH)

    nrow = [rows0 >> l for l in range(LEVELS)]
    ncol = [LANES >> l for l in range(LEVELS)]
    lane = lax.broadcasted_iota(jnp.int32, (depth, LANES), 1)
    level_z = lax.broadcasted_iota(jnp.int32, (depth, LANES), 0)
    nz = stage_s.shape[1]
    coef = jnp.concatenate([vert_ref[...], jnp.zeros((1, LANES - nz - 1), F32)], axis=1)
    coef = jnp.broadcast_to(coef, (depth, LANES))

    def down_lanes(shift):
        hit = (lane == level_z + shift) & (level_z < nz)
        return jnp.broadcast_to(jnp.sum(jnp.where(hit, coef, 0.0), axis=1, keepdims=True), (depth, LANES))

    up, down = down_lanes(1), down_lanes(0)
    kz_ref[0] = up
    kz_ref[1] = down
    kz_ref[2] = jnp.where(level_z < nz, 4.0 + up + down, 0.0)
    nblk, blk = inv_ref.shape[0], inv_ref.shape[1]
    for l in range(LEVELS):
        base[l] = jnp.zeros((depth, LANES), F32)
        for k in range(nblk):
            base[l, blk * k:blk * (k + 1), 0:blk] = inv_ref[k, :, l, :] * 0.0625
        block = base[l]
        full = block
        for k in range(1, nblk):
            full = jnp.where(level_z >= blk * k, pltpu.roll(block, blk * k, 1), full)
        hi, lo = split2(full)
        turned = pltpu.roll(hi, depth, 1)
        first = jnp.where(lane < depth, hi, turned)
        second = jnp.where(lane < 2 * depth - LANES, turned, pltpu.roll(lo, 2 * depth - LANES, 1))
        binv_ref[l] = jnp.concatenate([first, second], axis=1).astype(BF)
    flips = [flip_ref[0, 0, s] > 0 for s in range(4)]

    lane8 = lax.broadcasted_iota(jnp.int32, (8, LANES), 1)

    def restrict(row, l):
        both = row + pltpu.roll(row, LANES - 1, 1)
        return jnp.where(lane < ncol[l + 1], take(both, (2 * lane) & (LANES - 1)) * 0.25, 0.0)

    for l in range(LEVELS):
        for buf in (va[l], vb[l]):
            buf[0] = jnp.zeros((depth, LANES), F32)
            buf[nrow[l] + 1] = jnp.zeros((depth, LANES), F32)

    group = [4, 4, 3, 3]
    per_step = [8, 12, 6, 3]

    def each_group(l, body, carry=0):
        g = group[l] if nrow[l] % group[l] == 0 else 1
        step = per_step[l] if nrow[l] % per_step[l] == 0 else g

        def run(x0, acc):
            for off in range(0, step, g):
                acc = body(x0 + off, g, acc)
            return acc

        if step == nrow[l]:
            return run(0, carry)
        return lax.fori_loop(0, nrow[l] // step, lambda i, acc: run(i * step, acc), carry)

    def row_loop(n, step, body, carry=0):
        if n <= step or n % step:
            for i in range(n):
                carry = body(i, carry)
            return carry

        def run(t, acc):
            for j in range(step):
                acc = body(t * step + j, acc)
            return acc

        return lax.fori_loop(0, n // step, run, carry)

    def extract(acc, row, x, c):
        turned = pltpu.roll(row, 2 * x + 1, 1)
        hit = (lane == 2 * x + 1) | (lane == ((2 * x + c) & (LANES - 1)))
        return jnp.where(hit, turned, acc)

    def ends(c):
        return (lane == 0) | (lane == c - 1)

    def insert(tile, x, c):
        return jnp.where(ends(c), pltpu.roll(tile, (LANES - 1) - 2 * x, 1), 0.0)

    def row_size(l):
        return 8 * -(-(depth // 8) // FOLD_ROW[l])

    def end_size(l):
        return 8 * -(-(depth // 8) // FOLD_END[l])

    def put_ends(l, tile):
        edge[0:end_size(l)] = pack(tile, FOLD_END[l])

    def send(k, l, v):
        r = nrow[l]
        if l == 0:
            rows = (v.at[1], v.at[r])
        else:
            size = row_size(l)
            for side, at in ((0, 1), (1, r)):
                row_send[side, 0:size] = pack(jnp.where(lane < ncol[l], v[at], 0.0), FOLD_ROW[l])
            rows = (row_send.at[0, pl.ds(0, size)], row_send.at[1, pl.ds(0, size)])
        size = end_size(l)
        ends_ref = edge.at[pl.ds(0, size)]
        copies = []
        for ref, to, slot in ((rows[0], 0, 1), (rows[1], 1, 0), (ends_ref, 2, 3), (ends_ref, 3, 2)):
            count_z = row_size(l) if to < 2 else size
            copies.append(pltpu.make_async_remote_copy(
                src_ref=ref, dst_ref=held.at[k, slot, pl.ds(0, count_z)], send_sem=send_sem.at[k, slot],
                recv_sem=recv_sem.at[k, slot], device_id=peers[to], device_id_type=MESH))
            copies[-1].start()
        return copies

    def partial(l, v, x):
        c = ncol[l]
        mid = v[x + 1]
        r = src[l][x] - dia[l][x] * mid + (v[x] + v[x + 2])
        r = r + jnp.where(lane == 0, 0.0, pltpu.roll(mid, 1, 1))
        r = r + jnp.where(lane == c - 1, 0.0, pltpu.roll(mid, LANES - 1, 1))
        r = r + kz_ref[0] * pltpu.roll(mid, depth - 1, 0) + kz_ref[1] * pltpu.roll(mid, 1, 0)
        return r, mid

    def halos(k, l):
        r, c = nrow[l], ncol[l]
        size = row_size(l)
        low, high = (
            unpack(held[k, side, 0:size], jnp.where(flips[side], c - 1 - lane8, lane8), lane8 < c,
                   depth, FOLD_ROW[l])
            for side in range(2))
        size = end_size(l)
        odd = (lane8 & 1) == 1
        xm = lane8 >> 1
        xh = ((lane8 - c) & (LANES - 1)) >> 1
        from_low = 2 * jnp.where(flips[2], r - 1 - xm, xm) + c
        from_high = 2 * jnp.where(flips[3], r - 1 - xh, xh) + 1
        keep = jnp.where(odd, xm, xh) < r
        both = jnp.where((lane[0:size] & 1) == 1, held[k, 3, 0:size], held[k, 2, 0:size])
        beside = unpack(both, jnp.where(odd, from_low, from_high), keep, depth, FOLD_END[l])
        return low, high, beside

    count = [0]

    tail = jnp.zeros((depth - nz, LANES), F32)

    def first_field(v):
        acc = jnp.zeros((depth, LANES), F32)
        g = 4 if rows0 % 4 == 0 else 1
        for x0 in range(0, rows0, g):
            rows = []
            for x in range(x0, x0 + g):
                load_s[x].wait()
                rows.append(jnp.concatenate([stage_s[x] * 16.0, tail], axis=0))
                src[0][x] = rows[-1]
            d = block_dot(binv_ref[0, :, 0:3 * depth + 8], jnp.concatenate(rows, axis=1))
            for j in range(g):
                row = d[:, j * LANES:(j + 1) * LANES]
                v[x0 + j + 1] = row
                acc = extract(acc, row, x0 + j, ncol[0])
        put_ends(0, acc)

    def take_coef():
        for x in range(rows0):
            load_c[x].wait()
            dia[0][x] = jnp.concatenate([stage_c[x], tail], axis=0) + kz_ref[2]

    def coarse_coef():
        for l in range(LEVELS - 1):
            for x in range(nrow[l + 1]):
                dia[l + 1][x] = restrict(dia[l][2 * x] + dia[l][2 * x + 1], l)

    def from_zero(l, v):
        def body(x0, g, acc):
            rr = jnp.concatenate([src[l][x0 + j] for j in range(g)], axis=1)
            d = block_dot(binv_ref[l, :, 0:3 * depth + 8], rr)
            for j in range(g):
                row = d[:, j * LANES:(j + 1) * LANES]
                v[x0 + j + 1] = row
                acc = extract(acc, row, x0 + j, ncol[l])
            return acc
        put_ends(l, each_group(l, body, jnp.zeros((depth, LANES), F32)))

    def relax(l, v, w, pending=None, start=False):
        k = count[0]
        count[0] += 1
        copies = send(k, l, v)
        settle(l, v, pending)
        if start:
            take_coef()

        def body(x0, g, acc):
            parts = [partial(l, v, x0 + j) for j in range(g)]
            d = block_dot(binv_ref[l, :, 0:3 * depth + 8], jnp.concatenate([p[0] for p in parts], axis=1))
            for j in range(g):
                row = parts[j][1] + d[:, j * LANES:(j + 1) * LANES]
                w[x0 + j + 1] = row
                acc = extract(acc, row, x0 + j, ncol[l])
            return acc

        acc = each_group(l, body, jnp.zeros((depth, LANES), F32))
        if start:
            coarse_coef()
        for copy in copies:
            copy.wait()
        r, c = nrow[l], ncol[l]
        corr = block_dot(binv_ref[l, :, 0:3 * depth + 8], jnp.concatenate(halos(k, l), axis=1))
        low, high, beside = (corr[:, j * LANES:(j + 1) * LANES] for j in range(3))
        w[1] = w[1] + low + insert(beside, 0, c)
        w[r] = w[r] + high + insert(beside, r - 1, c)
        acc = acc + beside
        zero = jnp.zeros_like(acc)
        acc = acc + extract(zero, low, 0, c) + extract(zero, high, r - 1, c)
        put_ends(l, acc)
        return beside

    def settle(l, v, beside):
        if beside is None:
            return
        c = ncol[l]

        def body(i, acc):
            v[i + 2] = v[i + 2] + insert(beside, i + 1, c)
            return acc

        row_loop(nrow[l] - 2, 2 if nrow[l] > 6 else nrow[l], body)

    def residual(l, v, w, pending):
        k = count[0]
        count[0] += 1
        copies = send(k, l, v)
        settle(l, v, pending)

        def body(x0, g, acc):
            for j in range(g):
                w[x0 + j + 1] = partial(l, v, x0 + j)[0]
            return acc

        each_group(l, body)
        for copy in copies:
            copy.wait()
        r, c = nrow[l], ncol[l]
        low, high, beside = halos(k, l)
        w[1] = w[1] + low
        w[r] = w[r] + high

        def fold(i, acc):
            x = 2 * i
            pair = w[x + 1] + w[x + 2] + insert(beside, x, c) + insert(beside, x + 1, c)
            src[l + 1][i] = restrict(pair, l)
            return acc

        row_loop(r // 2, 3, fold)

    def add_coarse(l, v, coarse):
        def body(x, acc):
            fine = take(coarse[x + 1], lane >> 1)
            for j in (2 * x, 2 * x + 1):
                row = v[j + 1] + fine
                v[j + 1] = row
                acc = extract(acc, row, j, ncol[l])
            return acc

        put_ends(l, row_loop(nrow[l + 1], 3, body, jnp.zeros((depth, LANES), F32)))

    def cycle(l):
        a, b = va[l], vb[l]
        if l == 0:
            first_field(a)
            pl.semaphore_wait(barrier, 4)
        else:
            from_zero(l, a)
        if l == LEVELS - 1:
            p = relax(l, a, b)
            p = relax(l, b, a, p)
            p = relax(l, a, b, p)
            settle(l, b, p)
            return b
        p = relax(l, a, b, start=l == 0)
        residual(l, b, a, p)
        add_coarse(l, b, cycle(l + 1))
        p = relax(l, b, a)
        p = relax(l, a, b, p)
        settle(l, b, p)
        return b

    v = cycle(0)
    stores = []
    for x in range(rows0):
        stage_s[x] = v[x + 1][0:nz]
        stores.append(pltpu.make_async_copy(stage_s.at[x], out_ref.at[:, x, 0, :], io_sem.at[0, x]))
        stores[-1].start()
    for store in stores:
        store.wait()


def on_device(n_gx, n_gy, right_side, helm_coef, vert_coef, block_inverse, edge_flip):
    nz, rows, cols = right_side.shape
    depth = -(-nz // 8) * 8
    s, c = (a.reshape(nz, rows, 1, cols) for a in (right_side, helm_coef))
    vert = vert_coef.reshape(1, nz + 1)
    inv = block_inverse.transpose(1, 2, 0, 3)

    tile = lambda r: pltpu.VMEM((r, depth, LANES), F32)
    rl = [rows >> l for l in range(LEVELS)]
    steps = 4 * (LEVELS - 1) + 3
    hbm = pl.BlockSpec(memory_space=pl.ANY)
    vm = pl.BlockSpec(memory_space=pltpu.VMEM)
    out = pl.pallas_call(
        functools.partial(kernel, n_gx, n_gy, rows, depth),
        out_shape=jax.ShapeDtypeStruct((nz, rows, 1, LANES), F32),
        in_specs=[pl.BlockSpec(memory_space=pltpu.SMEM), hbm, hbm, vm, vm],
        out_specs=hbm,
        scratch_shapes=[
            pltpu.VMEM((rows, nz, LANES), F32),
            pltpu.VMEM((rows, nz, LANES), F32),
            pltpu.VMEM((2, depth, LANES), F32),
            pltpu.VMEM((3, depth, LANES), F32),
            pltpu.VMEM((LEVELS, depth, LANES), F32),
            pltpu.VMEM((LEVELS, depth, 2 * LANES), BF),
            pltpu.SemaphoreType.DMA((2, rows)),
        ] + [tile(r + 2) for r in rl] * 2 + [tile(r) for r in rl] * 2 + [
            pltpu.VMEM((depth, LANES), F32),
            pltpu.VMEM((steps, 4, depth, LANES), F32),
            pltpu.SemaphoreType.DMA((steps, 4)),
            pltpu.SemaphoreType.DMA((steps, 4)),
        ],
        compiler_params=pltpu.CompilerParams(
            collective_id=0, has_side_effects=True, vmem_limit_bytes=60 * 1024 * 1024),
    )(edge_flip, s, c, vert, inv)
    return out.reshape(nz, rows, cols)


def solution(mesh):
    placed = (P(None, "gx", "gy"), P(None, "gx", "gy"), P(), P(), P("gx", "gy", None))
    return jax.shard_map(
        functools.partial(on_device, mesh.shape["gx"], mesh.shape["gy"]),
        mesh=mesh, in_specs=placed, out_specs=P(None, "gx", "gy"), check_vma=False)
```

```python
import functools
import jax
import jax.numpy as jnp
from jax import lax
from jax.experimental import pallas as pl
from jax.experimental.pallas import tpu as pltpu
from jax.sharding import PartitionSpec as P

BLK = 14
LEVELS = 4
LANES = 128
MESH = pl.DeviceIdType.MESH
BF = jnp.bfloat16
F32 = jnp.float32


def split2(x):
    hi = x.astype(BF).astype(F32)
    return hi, x - hi


def take(tile, spot):
    return jnp.take_along_axis(tile, spot, axis=1, mode="promise_in_bounds")


FOLD_ROW = (1, 2, 4, 4)
FOLD_END = (2, 4, 4, 4)


def pack(tile, fold):
    width = LANES // fold
    units = tile.shape[0] // 8
    outs = []
    for first in range(0, units, fold):
        acc = tile[8 * first:8 * first + 8]
        for q in range(1, min(fold, units - first)):
            part = tile[8 * (first + q):8 * (first + q) + 8]
            acc = acc + pltpu.roll(part, width * q, 1)
        outs.append(acc)
    return jnp.concatenate(outs, axis=0)


def unpack(packed, spot, keep, depth, fold):
    parts = []
    for unit in range(depth // 8):
        j, q = divmod(unit, fold)
        at = (spot + q * (LANES // fold)) & (LANES - 1)
        parts.append(jnp.where(keep, take(packed[8 * j:8 * j + 8], at), 0.0))
    return jnp.concatenate(parts, axis=0)


def block_dot(binv, r):
    hi, lo = split2(r)
    cat = jnp.concatenate([hi, lo, hi, jnp.zeros((8, r.shape[1]), F32)], axis=0).astype(BF)
    return jnp.dot(binv, cat, preferred_element_type=F32)


def kernel(n_gx, n_gy, rows0, depth, flip_ref, s_in, c_in, vert_ref, inv_ref, out_ref,
           stage_s, stage_c, row_send, kz_ref, base, binv_ref, io_sem,
           va0, va1, va2, va3, vb0, vb1, vb2, vb3, s0, s1, s2, s3, d0, d1, d2, d3,
           edge, held, send_sem, recv_sem):
    va, vb = (va0, va1, va2, va3), (vb0, vb1, vb2, vb3)
    src, dia = (s0, s1, s2, s3), (d0, d1, d2, d3)
    gx, gy = lax.axis_index("gx"), lax.axis_index("gy")
    peers = (
        (lax.rem(gx + n_gx - 1, n_gx), gy),
        (lax.rem(gx + 1, n_gx), gy),
        (gx, lax.rem(gy + n_gy - 1, n_gy)),
        (gx, lax.rem(gy + 1, n_gy)),
    )
    load_s = [pltpu.make_async_copy(s_in.at[:, x, 0, :], stage_s.at[x], io_sem.at[0, x])
              for x in range(rows0)]
    load_c = [pltpu.make_async_copy(c_in.at[:, x, 0, :], stage_c.at[x], io_sem.at[1, x])
              for x in range(rows0)]
    for load in load_s + load_c:
        load.start()
    barrier = pltpu.get_barrier_semaphore()
    for peer in peers:
        pl.semaphore_signal(barrier, inc=1, device_id=peer, device_id_type=MESH)

    nrow = [rows0 >> l for l in range(LEVELS)]
    ncol = [LANES >> l for l in range(LEVELS)]
    lane = lax.broadcasted_iota(jnp.int32, (depth, LANES), 1)
    level_z = lax.broadcasted_iota(jnp.int32, (depth, LANES), 0)
    nz = stage_s.shape[1]
    coef = jnp.concatenate([vert_ref[...], jnp.zeros((1, LANES - nz - 1), F32)], axis=1)
    coef = jnp.broadcast_to(coef, (depth, LANES))

    def down_lanes(shift):
        hit = (lane == level_z + shift) & (level_z < nz)
        return jnp.broadcast_to(jnp.sum(jnp.where(hit, coef, 0.0), axis=1, keepdims=True), (depth, LANES))

    up, down = down_lanes(1), down_lanes(0)
    kz_ref[0] = up
    kz_ref[1] = down
    kz_ref[2] = jnp.where(level_z < nz, 4.0 + up + down, 0.0)
    nblk, blk = inv_ref.shape[0], inv_ref.shape[1]
    for l in range(LEVELS):
        base[l] = jnp.zeros((depth, LANES), F32)
        for k in range(nblk):
            base[l, blk * k:blk * (k + 1), 0:blk] = inv_ref[k, :, l, :] * 0.0625
        block = base[l]
        full = block
        for k in range(1, nblk):
            full = jnp.where(level_z >= blk * k, pltpu.roll(block, blk * k, 1), full)
        hi, lo = split2(full)
        turned = pltpu.roll(hi, depth, 1)
        first = jnp.where(lane < depth, hi, turned)
        second = jnp.where(lane < 2 * depth - LANES, turned, pltpu.roll(lo, 2 * depth - LANES, 1))
        binv_ref[l] = jnp.concatenate([first, second], axis=1).astype(BF)
    flips = [flip_ref[0, 0, s] > 0 for s in range(4)]

    lane8 = lax.broadcasted_iota(jnp.int32, (8, LANES), 1)

    def restrict(row, l):
        both = row + pltpu.roll(row, LANES - 1, 1)
        return jnp.where(lane < ncol[l + 1], take(both, (2 * lane) & (LANES - 1)) * 0.25, 0.0)

    for l in range(LEVELS):
        for buf in (va[l], vb[l]):
            buf[0] = jnp.zeros((depth, LANES), F32)
            buf[nrow[l] + 1] = jnp.zeros((depth, LANES), F32)

    group = [4, 4, 3, 3]
    per_step = [8, 12, 6, 3]

    def each_group(l, body, carry=0):
        g = group[l] if nrow[l] % group[l] == 0 else 1
        step = per_step[l] if nrow[l] % per_step[l] == 0 else g

        def run(x0, acc):
            for off in range(0, step, g):
                acc = body(x0 + off, g, acc)
            return acc

        if step == nrow[l]:
            return run(0, carry)
        return lax.fori_loop(0, nrow[l] // step, lambda i, acc: run(i * step, acc), carry)

    def row_loop(n, body, carry=0):
        for i in range(n):
            carry = body(i, carry)
        return carry

    def extract(acc, row, x, c):
        turned = pltpu.roll(row, 2 * x + 1, 1)
        hit = (lane == 2 * x + 1) | (lane == ((2 * x + c) & (LANES - 1)))
        return jnp.where(hit, turned, acc)

    def ends(c):
        return (lane == 0) | (lane == c - 1)

    def insert(tile, x, c):
        return jnp.where(ends(c), pltpu.roll(tile, (LANES - 1) - 2 * x, 1), 0.0)

    count = [0]
    leaving = []

    def row_size(l):
        return 8 * -(-(depth // 8) // FOLD_ROW[l])

    def end_size(l):
        return 8 * -(-(depth // 8) // FOLD_END[l])

    def put_ends(l, tile):
        edge[count[0] % 2, 0:end_size(l)] = pack(tile, FOLD_END[l])

    def send(k, l, v):
        r = nrow[l]
        if l == 0:
            rows = (v.at[1], v.at[r])
        else:
            size = row_size(l)
            for side, at in ((0, 1), (1, r)):
                row_send[k % 2, side, 0:size] = pack(jnp.where(lane < ncol[l], v[at], 0.0), FOLD_ROW[l])
            rows = (row_send.at[k % 2, 0, pl.ds(0, size)], row_send.at[k % 2, 1, pl.ds(0, size)])
        size = end_size(l)
        ends_ref = edge.at[k % 2, pl.ds(0, size)]
        copies = []
        for ref, to, slot in ((rows[0], 0, 1), (rows[1], 1, 0), (ends_ref, 2, 3), (ends_ref, 3, 2)):
            count_z = row_size(l) if to < 2 else size
            copies.append(pltpu.make_async_remote_copy(
                src_ref=ref, dst_ref=held.at[k, slot, pl.ds(0, count_z)], send_sem=send_sem.at[k, slot],
                recv_sem=recv_sem.at[k, slot], device_id=peers[to], device_id_type=MESH))
            copies[-1].start()
        for copy in leaving:
            copy.wait_send()
        leaving[:] = copies
        return copies

    def partial(l, v, x):
        c = ncol[l]
        mid = v[x + 1]
        r = src[l][x] - dia[l][x] * mid + (v[x] + v[x + 2])
        r = r + jnp.where(lane == 0, 0.0, pltpu.roll(mid, 1, 1))
        r = r + jnp.where(lane == c - 1, 0.0, pltpu.roll(mid, LANES - 1, 1))
        r = r + kz_ref[0] * pltpu.roll(mid, depth - 1, 0) + kz_ref[1] * pltpu.roll(mid, 1, 0)
        return r, mid

    def halos(k, l):
        r, c = nrow[l], ncol[l]
        size = row_size(l)
        low, high = (
            unpack(held[k, side, 0:size], jnp.where(flips[side], c - 1 - lane8, lane8), lane8 < c,
                   depth, FOLD_ROW[l])
            for side in range(2))
        size = end_size(l)
        odd = (lane8 & 1) == 1
        xm = lane8 >> 1
        xh = ((lane8 - c) & (LANES - 1)) >> 1
        from_low = 2 * jnp.where(flips[2], r - 1 - xm, xm) + c
        from_high = 2 * jnp.where(flips[3], r - 1 - xh, xh) + 1
        keep = jnp.where(odd, xm, xh) < r
        both = jnp.where((lane[0:size] & 1) == 1, held[k, 3, 0:size], held[k, 2, 0:size])
        beside = unpack(both, jnp.where(odd, from_low, from_high), keep, depth, FOLD_END[l])
        return low, high, beside


    tail = jnp.zeros((depth - nz, LANES), F32)

    def first_field(v):
        acc = jnp.zeros((depth, LANES), F32)
        g = 4 if rows0 % 4 == 0 else 1
        for x0 in range(0, rows0, g):
            rows = []
            for x in range(x0, x0 + g):
                load_s[x].wait()
                rows.append(jnp.concatenate([stage_s[x] * 16.0, tail], axis=0))
                src[0][x] = rows[-1]
            d = block_dot(binv_ref[0, :, 0:3 * depth + 8], jnp.concatenate(rows, axis=1))
            for j in range(g):
                row = d[:, j * LANES:(j + 1) * LANES]
                v[x0 + j + 1] = row
                acc = extract(acc, row, x0 + j, ncol[0])
        put_ends(0, acc)

    def take_coef():
        for x in range(rows0):
            load_c[x].wait()
            dia[0][x] = jnp.concatenate([stage_c[x], tail], axis=0) + kz_ref[2]

    def coarse_coef():
        for l in range(LEVELS - 1):
            for x in range(nrow[l + 1]):
                dia[l + 1][x] = restrict(dia[l][2 * x] + dia[l][2 * x + 1], l)

    def from_zero(l, v):
        def body(x0, g, acc):
            rr = jnp.concatenate([src[l][x0 + j] for j in range(g)], axis=1)
            d = block_dot(binv_ref[l, :, 0:3 * depth + 8], rr)
            for j in range(g):
                row = d[:, j * LANES:(j + 1) * LANES]
                v[x0 + j + 1] = row
                acc = extract(acc, row, x0 + j, ncol[l])
            return acc
        put_ends(l, each_group(l, body, jnp.zeros((depth, LANES), F32)))

    def relax(l, v, w, pending=None, start=False, last=False):
        k = count[0]
        count[0] += 1
        copies = send(k, l, v)
        settle(l, v, pending)
        if start:
            take_coef()

        def body(x0, g, acc):
            parts = [partial(l, v, x0 + j) for j in range(g)]
            d = block_dot(binv_ref[l, :, 0:3 * depth + 8], jnp.concatenate([p[0] for p in parts], axis=1))
            for j in range(g):
                row = parts[j][1] + d[:, j * LANES:(j + 1) * LANES]
                w[x0 + j + 1] = row
                if not last:
                    acc = extract(acc, row, x0 + j, ncol[l])
            return acc

        acc = each_group(l, body, jnp.zeros((depth, LANES), F32))
        if start:
            coarse_coef()
        for copy in copies:
            copy.wait_recv()
        r, c = nrow[l], ncol[l]
        corr = block_dot(binv_ref[l, :, 0:3 * depth + 8], jnp.concatenate(halos(k, l), axis=1))
        low, high, beside = (corr[:, j * LANES:(j + 1) * LANES] for j in range(3))
        w[1] = w[1] + low + insert(beside, 0, c)
        w[r] = w[r] + high + insert(beside, r - 1, c)
        if last:
            return beside
        acc = acc + beside
        zero = jnp.zeros_like(acc)
        acc = acc + extract(zero, low, 0, c) + extract(zero, high, r - 1, c)
        put_ends(l, acc)
        return beside

    def settle(l, v, beside):
        if beside is None:
            return
        c = ncol[l]

        def body(i, acc):
            v[i + 2] = v[i + 2] + insert(beside, i + 1, c)
            return acc

        row_loop(nrow[l] - 2, body)

    def residual(l, v, w, pending):
        k = count[0]
        count[0] += 1
        copies = send(k, l, v)
        settle(l, v, pending)

        def body(x0, g, acc):
            for j in range(g):
                w[x0 + j + 1] = partial(l, v, x0 + j)[0]
            return acc

        each_group(l, body)
        for copy in copies:
            copy.wait_recv()
        r, c = nrow[l], ncol[l]
        low, high, beside = halos(k, l)
        w[1] = w[1] + low
        w[r] = w[r] + high

        def fold(i, acc):
            x = 2 * i
            pair = w[x + 1] + w[x + 2] + insert(beside, x, c) + insert(beside, x + 1, c)
            src[l + 1][i] = restrict(pair, l)
            return acc

        row_loop(r // 2, fold)

    def add_coarse(l, v, coarse):
        def body(x, acc):
            fine = take(coarse[x + 1], lane >> 1)
            for j in (2 * x, 2 * x + 1):
                row = v[j + 1] + fine
                v[j + 1] = row
                acc = extract(acc, row, j, ncol[l])
            return acc

        put_ends(l, row_loop(nrow[l + 1], body, jnp.zeros((depth, LANES), F32)))

    def cycle(l):
        a, b = va[l], vb[l]
        if l == 0:
            first_field(a)
            pl.semaphore_wait(barrier, 4)
        else:
            from_zero(l, a)
        if l == LEVELS - 1:
            p = relax(l, a, b)
            p = relax(l, b, a, p)
            p = relax(l, a, b, p, last=True)
            settle(l, b, p)
            return b
        p = relax(l, a, b, start=l == 0)
        residual(l, b, a, p)
        add_coarse(l, b, cycle(l + 1))
        p = relax(l, b, a)
        p = relax(l, a, b, p, last=True)
        if l == 0:
            return b, p
        settle(l, b, p)
        return b

    v, rest = cycle(0)
    stores = []
    for x in range(rows0):
        row = v[x + 1]
        if 0 < x < rows0 - 1:
            row = row + insert(rest, x, ncol[0])
        stage_s[x] = row[0:nz]
        stores.append(pltpu.make_async_copy(stage_s.at[x], out_ref.at[:, x, 0, :], io_sem.at[0, x]))
        stores[-1].start()
    for copy in leaving:
        copy.wait_send()
    for store in stores:
        store.wait()


def on_device(n_gx, n_gy, right_side, helm_coef, vert_coef, block_inverse, edge_flip):
    nz, rows, cols = right_side.shape
    depth = -(-nz // 8) * 8
    s, c = (a.reshape(nz, rows, 1, cols) for a in (right_side, helm_coef))
    vert = vert_coef.reshape(1, nz + 1)
    inv = block_inverse.transpose(1, 2, 0, 3)

    tile = lambda r: pltpu.VMEM((r, depth, LANES), F32)
    rl = [rows >> l for l in range(LEVELS)]
    steps = 4 * (LEVELS - 1) + 3
    hbm = pl.BlockSpec(memory_space=pl.ANY)
    vm = pl.BlockSpec(memory_space=pltpu.VMEM)
    out = pl.pallas_call(
        functools.partial(kernel, n_gx, n_gy, rows, depth),
        out_shape=jax.ShapeDtypeStruct((nz, rows, 1, LANES), F32),
        in_specs=[pl.BlockSpec(memory_space=pltpu.SMEM), hbm, hbm, vm, vm],
        out_specs=hbm,
        scratch_shapes=[
            pltpu.VMEM((rows, nz, LANES), F32),
            pltpu.VMEM((rows, nz, LANES), F32),
            pltpu.VMEM((2, 2, depth, LANES), F32),
            pltpu.VMEM((3, depth, LANES), F32),
            pltpu.VMEM((LEVELS, depth, LANES), F32),
            pltpu.VMEM((LEVELS, depth, 2 * LANES), BF),
            pltpu.SemaphoreType.DMA((2, rows)),
        ] + [tile(r + 2) for r in rl] * 2 + [tile(r) for r in rl] * 2 + [
            pltpu.VMEM((2, depth, LANES), F32),
            pltpu.VMEM((steps, 4, depth, LANES), F32),
            pltpu.SemaphoreType.DMA((steps, 4)),
            pltpu.SemaphoreType.DMA((steps, 4)),
        ],
        compiler_params=pltpu.CompilerParams(
            collective_id=0, has_side_effects=True, vmem_limit_bytes=60 * 1024 * 1024),
    )(edge_flip, s, c, vert, inv)
    return out.reshape(nz, rows, cols)


def solution(mesh):
    placed = (P(None, "gx", "gy"), P(None, "gx", "gy"), P(), P(), P("gx", "gy", None))
    return jax.shard_map(
        functools.partial(on_device, mesh.shape["gx"], mesh.shape["gy"]),
        mesh=mesh, in_specs=placed, out_specs=P(None, "gx", "gy"), check_vma=False)
```

```python
import functools
import jax
import jax.numpy as jnp
from jax import lax
from jax.experimental import pallas as pl
from jax.experimental.pallas import tpu as pltpu
from jax.sharding import PartitionSpec as P

BLK = 14
LEVELS = 4
LANES = 128
MESH = pl.DeviceIdType.MESH
BF = jnp.bfloat16
F32 = jnp.float32


def split2(x):
    hi = x.astype(BF).astype(F32)
    return hi, x - hi


def take(tile, spot):
    return jnp.take_along_axis(tile, spot, axis=1, mode="promise_in_bounds")


FOLD_ROW = (1, 2, 4, 4)
FOLD_END = (2, 4, 4, 4)


def pack(tile, fold):
    width = LANES // fold
    units = tile.shape[0] // 8
    outs = []
    for first in range(0, units, fold):
        acc = tile[8 * first:8 * first + 8]
        for q in range(1, min(fold, units - first)):
            part = tile[8 * (first + q):8 * (first + q) + 8]
            acc = acc + pltpu.roll(part, width * q, 1)
        outs.append(acc)
    return jnp.concatenate(outs, axis=0)


def unpack(packed, spot, keep, depth, fold):
    parts = []
    for unit in range(depth // 8):
        j, q = divmod(unit, fold)
        at = (spot + q * (LANES // fold)) & (LANES - 1)
        parts.append(jnp.where(keep, take(packed[8 * j:8 * j + 8], at), 0.0))
    return jnp.concatenate(parts, axis=0)


def block_dot(binv, r):
    hi, lo = split2(r)
    cat = jnp.concatenate([hi, lo, hi, jnp.zeros((8, r.shape[1]), F32)], axis=0).astype(BF)
    return jnp.dot(binv, cat, preferred_element_type=F32)


def kernel(n_gx, n_gy, rows0, depth, flip_ref, s_in, c_in, vert_ref, inv_ref, out_ref,
           stage_s, stage_c, row_send, kz_ref, base, binv_ref, io_sem,
           va0, va1, va2, va3, vb0, vb1, vb2, vb3, s0, s1, s2, s3, d0, d1, d2, d3,
           edge, held, send_sem, recv_sem):
    va, vb = (va0, va1, va2, va3), (vb0, vb1, vb2, vb3)
    src, dia = (s0, s1, s2, s3), (d0, d1, d2, d3)
    gx, gy = lax.axis_index("gx"), lax.axis_index("gy")
    peers = (
        (lax.rem(gx + n_gx - 1, n_gx), gy),
        (lax.rem(gx + 1, n_gx), gy),
        (gx, lax.rem(gy + n_gy - 1, n_gy)),
        (gx, lax.rem(gy + 1, n_gy)),
    )
    load_s = [pltpu.make_async_copy(s_in.at[:, x, 0, :], stage_s.at[x], io_sem.at[0, x])
              for x in range(rows0)]
    load_c = [pltpu.make_async_copy(c_in.at[:, x, 0, :], stage_c.at[x], io_sem.at[1, x])
              for x in range(rows0)]
    for load in load_s + load_c:
        load.start()
    barrier = pltpu.get_barrier_semaphore()
    for peer in peers:
        pl.semaphore_signal(barrier, inc=1, device_id=peer, device_id_type=MESH)

    nrow = [rows0 >> l for l in range(LEVELS)]
    ncol = [LANES >> l for l in range(LEVELS)]
    lane = lax.broadcasted_iota(jnp.int32, (depth, LANES), 1)
    level_z = lax.broadcasted_iota(jnp.int32, (depth, LANES), 0)
    nz = stage_s.shape[1]
    coef = jnp.concatenate([vert_ref[...], jnp.zeros((1, LANES - nz - 1), F32)], axis=1)
    coef = jnp.broadcast_to(coef, (depth, LANES))

    def down_lanes(shift):
        hit = (lane == level_z + shift) & (level_z < nz)
        return jnp.broadcast_to(jnp.sum(jnp.where(hit, coef, 0.0), axis=1, keepdims=True), (depth, LANES))

    up, down = down_lanes(1), down_lanes(0)
    kz_ref[0] = up
    kz_ref[1] = down
    kz_ref[2] = jnp.where(level_z < nz, 4.0 + up + down, 0.0)
    nblk, blk = inv_ref.shape[0], inv_ref.shape[1]
    for l in range(LEVELS):
        base[l] = jnp.zeros((depth, LANES), F32)
        for k in range(nblk):
            base[l, blk * k:blk * (k + 1), 0:blk] = inv_ref[k, :, l, :] * 0.0625
        block = base[l]
        full = block
        for k in range(1, nblk):
            full = jnp.where(level_z >= blk * k, pltpu.roll(block, blk * k, 1), full)
        hi, lo = split2(full)
        turned = pltpu.roll(hi, depth, 1)
        first = jnp.where(lane < depth, hi, turned)
        second = jnp.where(lane < 2 * depth - LANES, turned, pltpu.roll(lo, 2 * depth - LANES, 1))
        binv_ref[l] = jnp.concatenate([first, second], axis=1).astype(BF)
    flips = [flip_ref[0, 0, s] > 0 for s in range(4)]

    lane8 = lax.broadcasted_iota(jnp.int32, (8, LANES), 1)

    def restrict(row, l):
        both = row + pltpu.roll(row, LANES - 1, 1)
        return jnp.where(lane < ncol[l + 1], take(both, (2 * lane) & (LANES - 1)) * 0.25, 0.0)

    for l in range(LEVELS):
        for buf in (va[l], vb[l]):
            buf[0] = jnp.zeros((depth, LANES), F32)
            buf[nrow[l] + 1] = jnp.zeros((depth, LANES), F32)

    group = [4, 4, 3, 3]
    per_step = [24, 12, 6, 3]

    def each_group(l, body, carry=0):
        g = group[l] if nrow[l] % group[l] == 0 else 1
        step = per_step[l] if nrow[l] % per_step[l] == 0 else g

        def run(x0, acc):
            for off in range(0, step, g):
                acc = body(x0 + off, g, acc)
            return acc

        if step == nrow[l]:
            return run(0, carry)
        return lax.fori_loop(0, nrow[l] // step, lambda i, acc: run(i * step, acc), carry)

    def row_loop(n, body, carry=0):
        for i in range(n):
            carry = body(i, carry)
        return carry

    def extract(acc, row, x, c):
        turned = pltpu.roll(row, 2 * x + 1, 1)
        hit = (lane == 2 * x + 1) | (lane == ((2 * x + c) & (LANES - 1)))
        return jnp.where(hit, turned, acc)

    def ends(c):
        return (lane == 0) | (lane == c - 1)

    def insert(tile, x, c):
        return jnp.where(ends(c), pltpu.roll(tile, (LANES - 1) - 2 * x, 1), 0.0)

    count = [0]
    leaving = []

    def row_size(l):
        return 8 * -(-(depth // 8) // FOLD_ROW[l])

    def end_size(l):
        return 8 * -(-(depth // 8) // FOLD_END[l])

    def put_ends(l, tile):
        edge[count[0] % 2, 0:end_size(l)] = pack(tile, FOLD_END[l])

    def send(k, l, v):
        r = nrow[l]
        if l == 0:
            rows = (v.at[1], v.at[r])
        else:
            size = row_size(l)
            for side, at in ((0, 1), (1, r)):
                row_send[k % 2, side, 0:size] = pack(jnp.where(lane < ncol[l], v[at], 0.0), FOLD_ROW[l])
            rows = (row_send.at[k % 2, 0, pl.ds(0, size)], row_send.at[k % 2, 1, pl.ds(0, size)])
        size = end_size(l)
        ends_ref = edge.at[k % 2, pl.ds(0, size)]
        copies = []
        for ref, to, slot in ((rows[0], 0, 1), (rows[1], 1, 0), (ends_ref, 2, 3), (ends_ref, 3, 2)):
            count_z = row_size(l) if to < 2 else size
            copies.append(pltpu.make_async_remote_copy(
                src_ref=ref, dst_ref=held.at[k, slot, pl.ds(0, count_z)], send_sem=send_sem.at[k, slot],
                recv_sem=recv_sem.at[k, slot], device_id=peers[to], device_id_type=MESH))
            copies[-1].start()
        for copy in leaving:
            copy.wait_send()
        leaving[:] = copies
        return copies

    def partial(l, v, x):
        c = ncol[l]
        mid = v[x + 1]
        r = src[l][x] - dia[l][x] * mid + (v[x] + v[x + 2])
        r = r + jnp.where(lane == 0, 0.0, pltpu.roll(mid, 1, 1))
        r = r + jnp.where(lane == c - 1, 0.0, pltpu.roll(mid, LANES - 1, 1))
        r = r + kz_ref[0] * pltpu.roll(mid, depth - 1, 0) + kz_ref[1] * pltpu.roll(mid, 1, 0)
        return r, mid

    def halos(k, l):
        r, c = nrow[l], ncol[l]
        size = row_size(l)
        low, high = (
            unpack(held[k, side, 0:size], jnp.where(flips[side], c - 1 - lane8, lane8), lane8 < c,
                   depth, FOLD_ROW[l])
            for side in range(2))
        size = end_size(l)
        odd = (lane8 & 1) == 1
        xm = lane8 >> 1
        xh = ((lane8 - c) & (LANES - 1)) >> 1
        from_low = 2 * jnp.where(flips[2], r - 1 - xm, xm) + c
        from_high = 2 * jnp.where(flips[3], r - 1 - xh, xh) + 1
        keep = jnp.where(odd, xm, xh) < r
        both = jnp.where((lane[0:size] & 1) == 1, held[k, 3, 0:size], held[k, 2, 0:size])
        beside = unpack(both, jnp.where(odd, from_low, from_high), keep, depth, FOLD_END[l])
        return low, high, beside


    tail = jnp.zeros((depth - nz, LANES), F32)

    def first_field(v):
        acc = jnp.zeros((depth, LANES), F32)
        g = 4 if rows0 % 4 == 0 else 1
        for x0 in range(0, rows0, g):
            rows = []
            for x in range(x0, x0 + g):
                load_s[x].wait()
                rows.append(jnp.concatenate([stage_s[x] * 16.0, tail], axis=0))
                src[0][x] = rows[-1]
            d = block_dot(binv_ref[0, :, 0:3 * depth + 8], jnp.concatenate(rows, axis=1))
            for j in range(g):
                row = d[:, j * LANES:(j + 1) * LANES]
                v[x0 + j + 1] = row
                acc = extract(acc, row, x0 + j, ncol[0])
        put_ends(0, acc)

    def take_coef():
        for x in range(rows0):
            load_c[x].wait()
            dia[0][x] = jnp.concatenate([stage_c[x], tail], axis=0) + kz_ref[2]

    def coarse_coef():
        for l in range(LEVELS - 1):
            for x in range(nrow[l + 1]):
                dia[l + 1][x] = restrict(dia[l][2 * x] + dia[l][2 * x + 1], l)

    def from_zero(l, v):
        def body(x0, g, acc):
            rr = jnp.concatenate([src[l][x0 + j] for j in range(g)], axis=1)
            d = block_dot(binv_ref[l, :, 0:3 * depth + 8], rr)
            for j in range(g):
                row = d[:, j * LANES:(j + 1) * LANES]
                v[x0 + j + 1] = row
                acc = extract(acc, row, x0 + j, ncol[l])
            return acc
        put_ends(l, each_group(l, body, jnp.zeros((depth, LANES), F32)))

    def relax(l, v, w, pending=None, start=False, last=False):
        k = count[0]
        count[0] += 1
        copies = send(k, l, v)
        settle(l, v, pending)
        if start:
            take_coef()

        def body(x0, g, acc):
            parts = [partial(l, v, x0 + j) for j in range(g)]
            d = block_dot(binv_ref[l, :, 0:3 * depth + 8], jnp.concatenate([p[0] for p in parts], axis=1))
            for j in range(g):
                row = parts[j][1] + d[:, j * LANES:(j + 1) * LANES]
                w[x0 + j + 1] = row
                if not last:
                    acc = extract(acc, row, x0 + j, ncol[l])
            return acc

        acc = each_group(l, body, jnp.zeros((depth, LANES), F32))
        if start:
            coarse_coef()
        for copy in copies:
            copy.wait_recv()
        r, c = nrow[l], ncol[l]
        corr = block_dot(binv_ref[l, :, 0:3 * depth + 8], jnp.concatenate(halos(k, l), axis=1))
        low, high, beside = (corr[:, j * LANES:(j + 1) * LANES] for j in range(3))
        w[1] = w[1] + low + insert(beside, 0, c)
        w[r] = w[r] + high + insert(beside, r - 1, c)
        if last:
            return beside
        acc = acc + beside
        zero = jnp.zeros_like(acc)
        acc = acc + extract(zero, low, 0, c) + extract(zero, high, r - 1, c)
        put_ends(l, acc)
        return beside

    def settle(l, v, beside):
        if beside is None:
            return
        c = ncol[l]

        def body(i, acc):
            v[i + 2] = v[i + 2] + insert(beside, i + 1, c)
            return acc

        row_loop(nrow[l] - 2, body)

    def residual(l, v, w, pending):
        k = count[0]
        count[0] += 1
        copies = send(k, l, v)
        settle(l, v, pending)

        def body(x0, g, acc):
            for j in range(g):
                w[x0 + j + 1] = partial(l, v, x0 + j)[0]
            return acc

        each_group(l, body)
        for copy in copies:
            copy.wait_recv()
        r, c = nrow[l], ncol[l]
        low, high, beside = halos(k, l)
        w[1] = w[1] + low
        w[r] = w[r] + high

        def fold(i, acc):
            x = 2 * i
            pair = w[x + 1] + w[x + 2] + insert(beside, x, c) + insert(beside, x + 1, c)
            src[l + 1][i] = restrict(pair, l)
            return acc

        row_loop(r // 2, fold)

    def add_coarse(l, v, coarse):
        def body(x, acc):
            fine = take(coarse[x + 1], lane >> 1)
            for j in (2 * x, 2 * x + 1):
                row = v[j + 1] + fine
                v[j + 1] = row
                acc = extract(acc, row, j, ncol[l])
            return acc

        put_ends(l, row_loop(nrow[l + 1], body, jnp.zeros((depth, LANES), F32)))

    def cycle(l):
        a, b = va[l], vb[l]
        if l == 0:
            first_field(a)
            pl.semaphore_wait(barrier, 4)
        else:
            from_zero(l, a)
        if l == LEVELS - 1:
            p = relax(l, a, b)
            p = relax(l, b, a, p)
            p = relax(l, a, b, p, last=True)
            settle(l, b, p)
            return b
        p = relax(l, a, b, start=l == 0)
        residual(l, b, a, p)
        add_coarse(l, b, cycle(l + 1))
        p = relax(l, b, a)
        p = relax(l, a, b, p, last=True)
        if l == 0:
            return b, p
        settle(l, b, p)
        return b

    v, rest = cycle(0)
    stores = []
    for x in range(rows0):
        row = v[x + 1]
        if 0 < x < rows0 - 1:
            row = row + insert(rest, x, ncol[0])
        stage_s[x] = row[0:nz]
        stores.append(pltpu.make_async_copy(stage_s.at[x], out_ref.at[:, x, 0, :], io_sem.at[0, x]))
        stores[-1].start()
    for copy in leaving:
        copy.wait_send()
    for store in stores:
        store.wait()


def on_device(n_gx, n_gy, right_side, helm_coef, vert_coef, block_inverse, edge_flip):
    nz, rows, cols = right_side.shape
    depth = -(-nz // 8) * 8
    s, c = (a.reshape(nz, rows, 1, cols) for a in (right_side, helm_coef))
    vert = vert_coef.reshape(1, nz + 1)
    inv = block_inverse.transpose(1, 2, 0, 3)

    tile = lambda r: pltpu.VMEM((r, depth, LANES), F32)
    rl = [rows >> l for l in range(LEVELS)]
    steps = 4 * (LEVELS - 1) + 3
    hbm = pl.BlockSpec(memory_space=pl.ANY)
    vm = pl.BlockSpec(memory_space=pltpu.VMEM)
    out = pl.pallas_call(
        functools.partial(kernel, n_gx, n_gy, rows, depth),
        out_shape=jax.ShapeDtypeStruct((nz, rows, 1, LANES), F32),
        in_specs=[pl.BlockSpec(memory_space=pltpu.SMEM), hbm, hbm, vm, vm],
        out_specs=hbm,
        scratch_shapes=[
            pltpu.VMEM((rows, nz, LANES), F32),
            pltpu.VMEM((rows, nz, LANES), F32),
            pltpu.VMEM((2, 2, depth, LANES), F32),
            pltpu.VMEM((3, depth, LANES), F32),
            pltpu.VMEM((LEVELS, depth, LANES), F32),
            pltpu.VMEM((LEVELS, depth, 2 * LANES), BF),
            pltpu.SemaphoreType.DMA((2, rows)),
        ] + [tile(r + 2) for r in rl] * 2 + [tile(r) for r in rl] * 2 + [
            pltpu.VMEM((2, depth, LANES), F32),
            pltpu.VMEM((steps, 4, depth, LANES), F32),
            pltpu.SemaphoreType.DMA((steps, 4)),
            pltpu.SemaphoreType.DMA((steps, 4)),
        ],
        compiler_params=pltpu.CompilerParams(
            collective_id=0, has_side_effects=True, vmem_limit_bytes=60 * 1024 * 1024),
    )(edge_flip, s, c, vert, inv)
    return out.reshape(nz, rows, cols)


def solution(mesh):
    placed = (P(None, "gx", "gy"), P(None, "gx", "gy"), P(), P(), P("gx", "gy", None))
    return jax.shard_map(
        functools.partial(on_device, mesh.shape["gx"], mesh.shape["gy"]),
        mesh=mesh, in_specs=placed, out_specs=P(None, "gx", "gy"), check_vma=False)
```
